32 devices in a mesh: ga: 4 (over z), ka: 8 (over y, x, core).
Axes of the slice: x: 2, y: 2, z: 4, core: 2. Of those that a mesh axis runs over, the one named last changes fastest.
Arguments:
- amplitudes: float32 [14400, 2048], P(None, ('ka', 'ga')), may hold values from -6 to 6
- integrals: float32 [2048, 15360], P('ga', 'ka'), may hold values from -0.125 to 0.125
Outputs:
- residual: float32 [14400, 15360], P('ga', 'ka')
The draws below stay inside these ranges and needn't reach their ends.
All inputs are finite; a program needn't handle non-finite values.
Results may differ from the reference program's by a relative error of at most 0.00007.
Values sent between devices are 32-bit elements; how exact they have to be, the bound alone decides.
No kernel may reach another device: no remote copies, remote signals or barrier semaphores. Data moves between devices by JAX's collectives and lax.ppermute only.
A program may use at most 128 MiB of HBM per device.

```python
import jax
import jax.numpy as jnp
from jax import lax

CD = 2048
IJ = 14400
AB = 15360


def level_of(own_key, shape, pieces, low, top_value):
    level = 1.0
    for position, blocks in pieces:
        heights = jax.random.uniform(jax.random.fold_in(jax.random.fold_in(own_key, 6), position), (blocks,), jnp.float32, low / len(pieces), top_value / len(pieces))
        level = level * jnp.repeat(jnp.exp(heights), shape[position] // blocks).reshape((-1,) + (1,) * (len(shape) - 1 - position))
    return level


def centred(own_key, extent, spread, reach, split=(), held_as=jnp.bfloat16):
    array = spread * jax.random.normal(own_key, extent, jnp.float32)
    if split:
        array = array * level_of(own_key, extent, split, -0.22, 0.18)
    return jnp.clip(array, -reach, reach).astype(held_as)


def setup_inputs(seed: int = 0) -> dict:
    key_list = jax.random.split(jax.random.key(seed), 3)
    amplitudes = centred(key_list[0], (IJ, CD), 1.0, 6.0, ((1, 32),), jnp.float32)
    integrals = centred(key_list[1], (CD, AB), CD ** -0.5, 0.125, ((0, 4), (1, 8)), jnp.float32)
    return {"amplitudes": amplitudes, "integrals": integrals}


def reference(amplitudes, integrals):
    ladder = jnp.dot(amplitudes, integrals, precision=lax.Precision.HIGHEST, preferred_element_type=jnp.float32)
    return 0.5 * ladder
```

```python
import functools

import jax
import jax.numpy as jnp
from jax import lax
from jax.experimental import pallas as pl
from jax.experimental.pallas import tpu as pltpu
from jax.sharding import PartitionSpec as P

ROWS = 240
WIDE = 512


def chunks_of(columns):
    wide = [(start, WIDE, WIDE) for start in range(0, columns - WIDE + 1, WIDE)]
    start = len(wide) * WIDE
    left = columns - start
    if left == 384:
        return [(start, 256, 256), *wide, (start + 256, 128, 128)]
    return wide + ([(start, left, WIDE)] if left else [])


def turn_kernel(t_ref, first_ref, second_ref):
    turned = t_ref[...].T
    half = turned.shape[1] // 2
    first_ref[...] = turned[:, :half]
    second_ref[...] = turned[:, half:]


def turn(columns):
    depth, rows = columns.shape
    width = 512
    half = jax.ShapeDtypeStruct((rows, depth // 2), jnp.float32)
    return pl.pallas_call(
        turn_kernel,
        grid=(pl.cdiv(rows, width),),
        in_specs=[pl.BlockSpec((depth, width), lambda i: (0, i))],
        out_specs=[pl.BlockSpec((width, depth // 2), lambda i: (i, 0))] * 2,
        out_shape=[half, half],
        cost_estimate=pl.CostEstimate(
            flops=0, bytes_accessed=8 * depth * rows, transcendentals=0
        ),
    )(columns)


def split(x):
    high = x.astype(jnp.bfloat16)
    return high, (x - high.astype(jnp.float32)).astype(jnp.bfloat16)


def product_kernel(blocks, place_ref, *refs):
    parts = refs[:blocks]
    w_ref = refs[blocks]
    out_ref, t_high, t_low, w_high, w_low = refs[-5:]
    half = parts[0].shape[1]

    @pl.when(pl.program_id(0) == 0)
    def _():
        for n in range(blocks // 2):
            start = pl.multiple_of((place_ref[0] ^ n) * 2 * half, 2 * half)
            high, low = split(w_ref[pl.ds(start, 2 * half), :])
            w_high[pl.ds(n * 2 * half, 2 * half), :] = high
            w_low[pl.ds(n * 2 * half, 2 * half), :] = low

    for n in range(blocks):
        high, low = split(parts[n][...])
        t_high[:, n * half : (n + 1) * half] = high
        t_low[:, n * half : (n + 1) * half] = low
    dot = functools.partial(jnp.dot, preferred_element_type=jnp.float32)
    total = dot(t_low[...], w_high[...])
    total += dot(t_high[...], w_low[...])
    total += dot(t_high[...], w_high[...])
    out_ref[:, : w_ref.shape[1]] = 0.5 * total


def product(place, parts, w, out, start, block, full):
    blocks = len(parts)
    rows, half = parts[0].shape
    depth, width = w.shape
    operands = [place, *parts, w]
    in_specs = [pl.BlockSpec((ROWS, half), lambda i, p: (i, 0))] * blocks
    in_specs.append(pl.BlockSpec((depth, width), lambda i, p: (0, 0)))
    aliases = {}
    if out is not None:
        aliases = {len(operands): 0}
        operands.append(out)
        in_specs.append(pl.BlockSpec(memory_space=pl.ANY))
    return pl.pallas_call(
        functools.partial(product_kernel, blocks),
        grid_spec=pltpu.PrefetchScalarGridSpec(
            num_scalar_prefetch=1,
            grid=(pl.cdiv(rows, ROWS),),
            in_specs=in_specs,
            out_specs=pl.BlockSpec((ROWS, block), lambda i, p: (i, start // block)),
            scratch_shapes=[
                pltpu.VMEM((ROWS, depth), jnp.bfloat16),
                pltpu.VMEM((ROWS, depth), jnp.bfloat16),
                pltpu.VMEM((depth, width), jnp.bfloat16),
                pltpu.VMEM((depth, width), jnp.bfloat16),
            ],
        ),
        out_shape=jax.ShapeDtypeStruct((rows, full), jnp.float32),
        input_output_aliases=aliases,
        compiler_params=pltpu.CompilerParams(vmem_limit_bytes=40 * 2**20),
        cost_estimate=pl.CostEstimate(
            flops=6 * rows * depth * width,
            bytes_accessed=4 * (rows * depth + depth * width + rows * width),
            transcendentals=0,
        ),
    )(*operands)


def per_device(devices, amplitudes, integrals):
    swap = lambda x, mask: lax.ppermute(x, "ka", [(d, d ^ mask) for d in range(devices)])
    regrouped = lax.all_to_all(amplitudes, "ga", split_axis=0, concat_axis=1, tiled=True)
    chunks = chunks_of(integrals.shape[1])

    def gather(chunk, source):
        piece = lax.slice_in_dim(source, chunk[0], chunk[0] + chunk[1], axis=1)
        return lax.all_gather(piece, "ga", axis=0, tiled=True)

    pieces = [gather(chunks[0], integrals)]
    regrouped, later = lax.optimization_barrier((regrouped, integrals))
    pieces += [gather(chunk, later) for chunk in chunks[1:]]

    masks = [1 << bit for bit in range(1, devices.bit_length() - 1)]
    halves = []
    for half, order in zip(turn(regrouped.T), (masks[::-1], masks)):
        held = {0: half}
        for mask in (*order, 1):
            held |= {n ^ mask: swap(block, mask) for n, block in held.items()}
        halves.append(held)
    parts = [held[n] for n in range(devices) for held in halves]

    place = lax.axis_index("ka").astype(jnp.int32).reshape(1)
    out = None
    for (start, _, block), piece in zip(chunks, pieces):
        out = product(place, parts, piece, out, start, block, integrals.shape[1])
    return out


def solution(mesh):
    placed = (P(None, ("ka", "ga")), P("ga", "ka"))
    return jax.shard_map(
        functools.partial(per_device, mesh.shape["ka"]),
        mesh=mesh,
        in_specs=placed,
        out_specs=P("ga", "ka"),
        check_vma=False,
    )
```

```python
import functools

import jax
import jax.numpy as jnp
from jax import lax
from jax.experimental import pallas as pl
from jax.experimental.pallas import tpu as pltpu
from jax.sharding import PartitionSpec as P

ROWS = 720
WIDE = 512
VMEM_BYTES = 60 * 2**20


def params():
    return pltpu.CompilerParams(vmem_limit_bytes=VMEM_BYTES)


def moved(bytes_accessed, flops=0):
    return pl.CostEstimate(
        flops=flops, bytes_accessed=bytes_accessed, transcendentals=0
    )


def chunks_of(columns, line):
    if columns == 1920 and line == 4:
        return [
            (1024, 256, 256, False),
            (0, 512, 512, False),
            (512, 512, 512, False),
            (1536, 384, 384, True),
            (1280, 256, 256, False),
        ]
    wide = [(n, WIDE, WIDE, False) for n in range(0, columns - WIDE + 1, WIDE)]
    start = len(wide) * WIDE
    return wide + ([(start, columns - start, WIDE, False)] if start < columns else [])


def holder(here, n):
    away = here ^ n
    if away < 2:
        return away
    if here in (0, 3):
        return 3 if away == 2 else 5
    return 4 if away == 2 else 2


def along_line(own):
    inner, outer = [(1, 2), (2, 1)], [(1, 0), (2, 3)]
    send = lambda x, pairs: lax.ppermute(x, "ga", pairs)
    first = send(own, outer + [(0, 1), (3, 2)])
    second = send(own, inner)
    fourth = send(first, inner)
    third = send(second, outer)
    fifth = send(fourth, outer)
    return [own, first, second, third, fourth, fifth]


def cut_kernel(t_ref, out_ref):
    groups, _, rows = out_ref.shape
    for n in range(groups):
        out_ref[n] = t_ref[:, n * rows : (n + 1) * rows]


def cut(columns, groups, half):
    depth, pairs = columns.shape
    shape = (groups, depth // 2, pairs // groups)
    return pl.pallas_call(
        cut_kernel,
        grid=(1,),
        in_specs=[pl.BlockSpec((depth // 2, pairs), lambda i: (half, 0))],
        out_specs=pl.BlockSpec(shape, lambda i: (0, 0, 0)),
        out_shape=jax.ShapeDtypeStruct(shape, jnp.float32),
        compiler_params=params(),
        cost_estimate=moved(4 * depth * pairs),
    )(columns)


def turn_kernel(t_ref, out_ref):
    out_ref[...] = t_ref[...].T


def turn(columns):
    depth, rows = columns.shape
    width = 1024
    return pl.pallas_call(
        turn_kernel,
        grid=(pl.cdiv(rows, width),),
        in_specs=[pl.BlockSpec((depth, width), lambda i: (0, i))],
        out_specs=pl.BlockSpec((width, depth), lambda i: (i, 0)),
        out_shape=jax.ShapeDtypeStruct((rows, depth), jnp.float32),
        compiler_params=params(),
        cost_estimate=moved(8 * depth * rows),
    )(columns)


def split(x):
    high = x.astype(jnp.bfloat16)
    return high, (x - high.astype(jnp.float32)).astype(jnp.bfloat16)


def halve_kernel(blocks, *refs):
    high_ref, low_ref = refs[-2:]
    width = refs[0].shape[1]
    for n in range(blocks):
        high, low = split(refs[n][...])
        high_ref[:, n * width : (n + 1) * width] = high
        low_ref[:, n * width : (n + 1) * width] = low


def halve(parts, held, group, depth):
    blocks = len(parts)
    rows, width = parts[0].shape
    whole = jax.ShapeDtypeStruct((rows, depth), jnp.bfloat16)
    in_specs = [pl.BlockSpec((ROWS, width), lambda i: (i, 0))] * blocks
    in_specs += [pl.BlockSpec(memory_space=pl.ANY)] * len(held)
    out_spec = pl.BlockSpec((ROWS, width * blocks), lambda i: (i, group))
    return pl.pallas_call(
        functools.partial(halve_kernel, blocks),
        grid=(pl.cdiv(rows, ROWS),),
        in_specs=in_specs,
        out_specs=[out_spec, out_spec],
        out_shape=[whole, whole],
        input_output_aliases={blocks + n: n for n in range(len(held))},
        compiler_params=params(),
        cost_estimate=moved(8 * rows * width * blocks),
    )(*parts, *held)


def product_kernel(line, devices, gathered, place_ref, t_high, t_low, *refs):
    out_ref, w, w_high, w_low, arrived = refs[-5:]
    depth, width = w.shape
    size = depth // line

    @pl.when(pl.program_id(0) == 0)
    def _():
        if gathered:
            whole = pltpu.make_async_copy(refs[0], w, arrived.at[0])
            whole.start()
            whole.wait()
        else:

            def copy(source, n):
                return pltpu.make_async_copy(
                    refs[source], w.at[pl.ds(n * size, size)], arrived.at[n]
                )

            for here in range(line):

                @pl.when(place_ref[1] == here)
                def _():
                    for n in range(line):
                        copy(holder(here, n), n).start()

            for n in range(line):
                copy(0, n).wait()
        block = depth // devices
        piece = block // line // 2
        for n in range(devices):
            start = (place_ref[0] ^ n) * block
            for half in range(2):
                rows = [
                    w[pl.ds(pl.multiple_of(start, block) + (2 * m + half) * piece, piece), :]
                    for m in range(line)
                ]
                high, low = split(jnp.concatenate(rows, axis=0))
                to = pl.ds((2 * n + half) * (block // 2), block // 2)
                w_high[to, :] = high
                w_low[to, :] = low

    dot = functools.partial(jnp.dot, preferred_element_type=jnp.float32)
    total = dot(t_low[...], w_high[...])
    total += dot(t_high[...], w_low[...])
    total += dot(t_high[...], w_high[...])
    out_ref[:, :width] = 0.5 * total


def product(line, devices, place, t_high, t_low, shards, out, chunk, full):
    start, width, block, by_line = chunk
    rows, depth = t_high.shape
    t_spec = pl.BlockSpec((ROWS, depth), lambda i, p: (i, 0))
    anywhere = pl.BlockSpec(memory_space=pl.ANY)
    operands = [place, t_high, t_low, *shards]
    aliases = {}
    if out is not None:
        aliases = {len(operands): 0}
        operands.append(out)
    return pl.pallas_call(
        functools.partial(product_kernel, line, devices, not by_line),
        grid_spec=pltpu.PrefetchScalarGridSpec(
            num_scalar_prefetch=1,
            grid=(pl.cdiv(rows, ROWS),),
            in_specs=[t_spec, t_spec] + [anywhere] * (len(operands) - 3),
            out_specs=pl.BlockSpec((ROWS, block), lambda i, p: (i, start // block)),
            scratch_shapes=[
                pltpu.VMEM((depth, width), jnp.float32),
                pltpu.VMEM((depth, width), jnp.bfloat16),
                pltpu.VMEM((depth, width), jnp.bfloat16),
                pltpu.SemaphoreType.DMA((line,)),
            ],
        ),
        out_shape=jax.ShapeDtypeStruct((rows, full), jnp.float32),
        input_output_aliases=aliases,
        compiler_params=params(),
        cost_estimate=moved(
            4 * (rows * depth + depth * width + rows * width),
            6 * rows * depth * width,
        ),
    )(*operands)


def after(value, *others):
    return lax.optimization_barrier((value, *others))[0]


def per_device(line, devices, amplitudes, integrals):
    columns = integrals.shape[1]
    depth = integrals.shape[0] * line

    chunks = chunks_of(columns, line)

    def piece(chunk, source):
        return lax.slice_in_dim(source, chunk[0], chunk[0] + chunk[1], axis=1)

    def gather(x):
        return [lax.all_gather(x, "ga", axis=0, tiled=True)]

    first, amplitudes = lax.optimization_barrier((piece(chunks[0], integrals), amplitudes))
    shards = {chunks[0]: gather(first)}
    for chunk in chunks[1:]:
        if not chunk[3]:
            shards[chunk] = gather(piece(chunk, integrals))

    regrouped = []
    for half in range(2):
        blocks = cut(amplitudes.T, line, half)
        blocks = lax.all_to_all(blocks, "ga", split_axis=0, concat_axis=0, tiled=True)
        regrouped.append(blocks.reshape(-1, blocks.shape[-1]))
    regrouped[1] = after(regrouped[1], *shards[chunks[0]])

    def swap(x, mask):
        return lax.ppermute(x, "ka", [(d, d ^ mask) for d in range(devices)])

    masks = [1 << bit for bit in range(1, devices.bit_length() - 1)]
    halves = []
    for half, order in zip(regrouped, (masks[::-1], masks)):
        held = {0: turn(half)}
        for mask in (*order, 1):
            held |= {n ^ mask: swap(block, mask) for n, block in held.items()}
        halves.append(held)

    rest = after(integrals, halves[0][devices - 2], halves[1][devices - 2])
    shards |= {chunk: along_line(piece(chunk, rest)) for chunk in chunks if chunk[3]}

    whole = ()
    for group in range(devices // 2):
        parts = [held[n] for n in (2 * group, 2 * group + 1) for held in halves]
        whole = halve(parts, whole, group, depth)

    place = jnp.stack([lax.axis_index("ka"), lax.axis_index("ga")])
    moving = [shards[chunk] for chunk in chunks if chunk[3]]
    out = None
    for n, chunk in enumerate(chunks):
        if moving and n in (1, 2):
            out = after(out, *moving[0][2 * n - 1 : 2 * n + 1])
        out = product(line, devices, place, *whole, shards[chunk], out, chunk, columns)
    return out


def solution(mesh):
    placed = (P(None, ("ka", "ga")), P("ga", "ka"))
    return jax.shard_map(
        functools.partial(per_device, mesh.shape["ga"], mesh.shape["ka"]),
        mesh=mesh,
        in_specs=placed,
        out_specs=P("ga", "ka"),
        check_vma=False,
    )
```

```python
import functools

import jax
import jax.numpy as jnp
from jax import lax
from jax.experimental import pallas as pl
from jax.experimental.pallas import tpu as pltpu
from jax.sharding import PartitionSpec as P

ROWS = 240
WIDE = 512
VMEM_BYTES = 60 * 2**20


def params():
    return pltpu.CompilerParams(vmem_limit_bytes=VMEM_BYTES)


def moved(bytes_accessed, flops=0):
    return pl.CostEstimate(
        flops=flops, bytes_accessed=bytes_accessed, transcendentals=0
    )


def chunks_of(columns, line):
    if columns == 1920 and line == 4:
        return [
            (768, 256, 256, False),
            (0, 512, 512, True),
            (1536, 384, 384, False),
            (1024, 256, 256, False),
            (512, 256, 256, True),
            (1280, 256, 256, False),
        ]
    wide = [(n, WIDE, WIDE, False) for n in range(0, columns - WIDE + 1, WIDE)]
    start = len(wide) * WIDE
    return wide + ([(start, columns - start, WIDE, False)] if start < columns else [])


def cut_kernel(first, rows, t_ref, out_ref):
    groups, _, taken = out_ref.shape
    for n in range(groups):
        start = n * rows + first
        out_ref[n] = t_ref[:, start : start + taken]


def cut(columns, groups, first, taken):
    depth, pairs = columns.shape
    shape = (groups, depth, taken)
    return pl.pallas_call(
        functools.partial(cut_kernel, first, pairs // groups),
        grid=(1,),
        in_specs=[pl.BlockSpec((depth, pairs), lambda i: (0, 0))],
        out_specs=pl.BlockSpec(shape, lambda i: (0, 0, 0)),
        out_shape=jax.ShapeDtypeStruct(shape, jnp.float32),
        compiler_params=params(),
        cost_estimate=moved(6 * depth * pairs),
    )(columns)


def turn_kernel(t_ref, out_ref):
    out_ref[...] = t_ref[...].T


def turn(columns):
    depth, rows = columns.shape
    width = 512
    return pl.pallas_call(
        turn_kernel,
        grid=(pl.cdiv(rows, width),),
        in_specs=[pl.BlockSpec((depth, width), lambda i: (0, i))],
        out_specs=pl.BlockSpec((width, depth), lambda i: (i, 0)),
        out_shape=jax.ShapeDtypeStruct((rows, depth), jnp.float32),
        compiler_params=params(),
        cost_estimate=moved(8 * depth * rows),
    )(columns)


def split(x):
    high = x.astype(jnp.bfloat16)
    return high, (x - high.astype(jnp.float32)).astype(jnp.bfloat16)


def holder(here, n):
    away = here ^ n
    if away < 2:
        return away
    if here in (0, 3):
        return 3 if away == 2 else 5
    return 4 if away == 2 else 2


def product_kernel(line, devices, gathered, place_ref, *refs):
    out_ref, w, t_three, w_three, arrived = refs[-5:]
    parts, sources = refs[:devices], refs[devices:]
    depth, width = w.shape
    size = depth // line
    block = depth // devices

    @pl.when(pl.program_id(0) == 0)
    def _():
        if gathered:
            whole = pltpu.make_async_copy(sources[0], w, arrived.at[0])
            whole.start()
            whole.wait()
        else:

            def copy(source, n):
                return pltpu.make_async_copy(
                    sources[source], w.at[pl.ds(n * size, size)], arrived.at[n]
                )

            for here in range(line):

                @pl.when(place_ref[1] == here)
                def _():
                    for n in range(line):
                        copy(holder(here, n), n).start()

            for n in range(line):
                copy(0, n).wait()
        for n in range(devices):
            start = pl.multiple_of((place_ref[0] ^ n) * block, block)
            high, low = split(w[pl.ds(start, block), :])
            for third, value in enumerate((high, high, low)):
                w_three[pl.ds(third * depth + n * block, block), :] = value

    for n in range(devices):
        high, low = split(parts[n][...])
        for third, value in enumerate((low, high, high)):
            start = third * depth + n * block
            t_three[:, start : start + block] = value
    total = jnp.dot(t_three[...], w_three[...], preferred_element_type=jnp.float32)
    out_ref[:, :width] = 0.5 * total


def product(line, place, parts, sources, out, chunk, first, shape):
    start, width, block, by_line = chunk
    devices = len(parts)
    rows, size = parts[0].shape
    depth = size * devices
    part_spec = pl.BlockSpec((ROWS, size), lambda i, p: (i, 0))
    anywhere = pl.BlockSpec(memory_space=pl.ANY)
    operands = [place, *parts, *sources]
    aliases = {}
    if out is not None:
        aliases = {len(operands): 0}
        operands.append(out)
    return pl.pallas_call(
        functools.partial(product_kernel, line, devices, not by_line),
        grid_spec=pltpu.PrefetchScalarGridSpec(
            num_scalar_prefetch=1,
            grid=(pl.cdiv(rows, ROWS),),
            in_specs=[part_spec] * devices + [anywhere] * (len(operands) - 1 - devices),
            out_specs=pl.BlockSpec(
                (ROWS, block), lambda i, p: (first // ROWS + i, start // block)
            ),
            scratch_shapes=[
                pltpu.VMEM((depth, width), jnp.float32),
                pltpu.VMEM((ROWS, 3 * depth), jnp.bfloat16),
                pltpu.VMEM((3 * depth, width), jnp.bfloat16),
                pltpu.SemaphoreType.DMA((line,)),
            ],
        ),
        out_shape=jax.ShapeDtypeStruct(shape, jnp.float32),
        input_output_aliases=aliases,
        compiler_params=params(),
        cost_estimate=moved(
            4 * (rows * depth + depth * width + rows * width),
            6 * rows * depth * width,
        ),
    )(*operands)


def after(value, *others):
    return lax.optimization_barrier((value, *others))[0]


def per_device(line, devices, amplitudes, integrals):
    columns = integrals.shape[1]
    rows = amplitudes.shape[0] // line
    chunks = chunks_of(columns, line)
    outer, inner = [(1, 0), (2, 3)], [(1, 2), (2, 1)]

    def piece(chunk, source):
        return lax.slice_in_dim(source, chunk[0], chunk[0] + chunk[1], axis=1)

    def send(x, pairs):
        return lax.ppermute(x, "ga", pairs)

    def swap(x, mask):
        return lax.ppermute(x, "ka", [(d, d ^ mask) for d in range(devices)])

    moving = [chunk for chunk in chunks if chunk[3]]
    sources = {}
    for chunk in moving[:1]:
        own = piece(chunk, integrals)
        sources[chunk] = [own, send(own, outer + [(0, 1), (3, 2)])]

    tiles = pl.cdiv(rows, ROWS)
    middle = (tiles + 1) // 2 * ROWS
    bounds = ((0, middle), (middle, rows - middle))
    regrouped = []
    for first, taken in bounds:
        blocks = cut(amplitudes.T, line, first, taken)
        blocks = lax.all_to_all(blocks, "ga", split_axis=0, concat_axis=0, tiled=True)
        regrouped.append(blocks.reshape(-1, taken))
    regrouped[0] = after(regrouped[0], *[sources[chunk][1] for chunk in moving[:1]])

    rest = after(integrals, regrouped[1])
    for chunk in chunks:
        if not chunk[3]:
            own = piece(chunk, rest)
            sources[chunk] = [lax.all_gather(own, "ga", axis=0, tiled=True)]

    masks = [1 << bit for bit in range(1, devices.bit_length() - 1)]
    halves = []
    for half, order in zip(regrouped, (masks[::-1], masks)):
        held = {0: turn(half)}
        for level in range(1, len(masks) + 1):
            ready, _ = lax.optimization_barrier((held, regrouped[1] if level > 1 else ()))
            for n in range(2, devices, 2):
                if n.bit_count() == level:
                    last = [mask for mask in order if n & mask][-1]
                    held[n] = swap(ready[n ^ last], last)
        halves.append(held)
    halves[0] |= {n ^ 1: swap(block, 1) for n, block in halves[0].items()}

    steps = {}
    if moving:
        near, far = moving
        diagonal = halves[0][devices - 2]
        own, first = sources[near]
        second = send(after(own, regrouped[1]), inner)
        first, ready = lax.optimization_barrier((first, (second, diagonal)))
        third, fourth = send(ready[0], outer), send(first, inner)
        sources[near] += [second, third, fourth, None]
        sources[far] = [None] * 6

        def step_2(out):
            out, own = lax.optimization_barrier((out, piece(far, integrals)))
            sources[far][:3] = own, send(own, outer + [(0, 1), (3, 2)]), send(own, inner)
            return out

        def step_4(out):
            out, last = lax.optimization_barrier((out, sources[far][1:3]))
            sources[far][3:5] = send(last[1], outer), send(last[0], inner)
            return out

        def step_6(out):
            out, last = lax.optimization_barrier((out, sources[far][3:5]))
            sources[far][5] = send(last[1], outer)
            return out

        steps = {2: step_2, 4: step_4, 6: step_6}

    def step_1(out):
        early = {n: block for n, block in halves[1].items() if n != devices - 2}
        last = [third, fourth] if moving else []
        out, early, last = lax.optimization_barrier((out, early, last))
        halves[1] |= {n ^ 1: swap(block, 1) for n, block in early.items()}
        if moving:
            sources[near][5] = send(last[1], outer)
        out, corner = lax.optimization_barrier((out, halves[1][devices - 2]))
        halves[1][devices - 1] = swap(corner, 1)
        return out

    steps[1] = step_1

    place = jnp.stack([lax.axis_index("ka"), lax.axis_index("ga")])
    out = None
    calls = [(chunk, half) for chunk in chunks for half in range(2)]
    for n, (chunk, half) in enumerate(calls):
        if n in steps:
            out = steps[n](out)
        out = product(
            line,
            place,
            [halves[half][m] for m in range(devices)],
            sources[chunk],
            out,
            chunk,
            bounds[half][0],
            (rows, columns),
        )
    return out


def solution(mesh):
    placed = (P(None, ("ka", "ga")), P("ga", "ka"))
    return jax.shard_map(
        functools.partial(per_device, mesh.shape["ga"], mesh.shape["ka"]),
        mesh=mesh,
        in_specs=placed,
        out_specs=P("ga", "ka"),
        check_vma=False,
    )
```

```python
import functools

import jax
import jax.numpy as jnp
from jax import lax
from jax.experimental import pallas as pl
from jax.experimental.pallas import tpu as pltpu
from jax.sharding import PartitionSpec as P

ROWS = 400
WIDE = 512
VMEM_BYTES = 60 * 2**20


def params():
    return pltpu.CompilerParams(vmem_limit_bytes=VMEM_BYTES)


def moved(bytes_accessed, flops=0):
    return pl.CostEstimate(
        flops=flops, bytes_accessed=bytes_accessed, transcendentals=0
    )


def chunks_of(columns, line):
    if columns == 1920 and line == 4:
        return [
            (768, 256, 256, False),
            (0, 512, 512, True),
            (1536, 384, 384, False),
            (1024, 256, 256, False),
            (512, 256, 256, True),
            (1280, 256, 256, False),
        ]
    wide = [(n, WIDE, WIDE, False) for n in range(0, columns - WIDE + 1, WIDE)]
    start = len(wide) * WIDE
    return wide + ([(start, columns - start, WIDE, False)] if start < columns else [])


def cut_kernel(t_ref, out_ref):
    groups, _, rows = out_ref.shape
    for n in range(groups):
        out_ref[n] = t_ref[:, n * rows : (n + 1) * rows]


def cut(columns, groups, half):
    depth, pairs = columns.shape
    shape = (groups, depth // 2, pairs // groups)
    return pl.pallas_call(
        cut_kernel,
        grid=(1,),
        in_specs=[pl.BlockSpec((depth // 2, pairs), lambda i: (half, 0))],
        out_specs=pl.BlockSpec(shape, lambda i: (0, 0, 0)),
        out_shape=jax.ShapeDtypeStruct(shape, jnp.float32),
        compiler_params=params(),
        cost_estimate=moved(4 * depth * pairs),
    )(columns)


def turn_kernel(t_ref, out_ref):
    out_ref[...] = t_ref[...].T


def turn(columns):
    depth, rows = columns.shape
    width = 512
    return pl.pallas_call(
        turn_kernel,
        grid=(pl.cdiv(rows, width),),
        in_specs=[pl.BlockSpec((depth, width), lambda i: (0, i))],
        out_specs=pl.BlockSpec((width, depth), lambda i: (i, 0)),
        out_shape=jax.ShapeDtypeStruct((rows, depth), jnp.float32),
        compiler_params=params(),
        cost_estimate=moved(8 * depth * rows),
    )(columns)


def split(x):
    high = x.astype(jnp.bfloat16)
    return high, (x - high.astype(jnp.float32)).astype(jnp.bfloat16)


def holder(here, n):
    away = here ^ n
    if away < 2:
        return away
    if here in (0, 3):
        return 3 if away == 2 else 5
    return 4 if away == 2 else 2


def product_kernel(line, devices, gathered, place_ref, *refs):
    out_ref, w, w_high, w_low, even_high, even_low, odd_high, odd_low, arrived = refs[-9:]
    parts, sources = refs[: 2 * devices], refs[2 * devices :]
    depth, width = w.shape
    size = depth // line
    block = depth // devices
    half = block // 2
    now = pl.program_id(0)

    @pl.when(now == 0)
    def _():
        if gathered:
            whole = pltpu.make_async_copy(sources[0], w, arrived.at[0])
            whole.start()
            whole.wait()
        else:

            def copy(source, n):
                return pltpu.make_async_copy(
                    sources[source], w.at[pl.ds(n * size, size)], arrived.at[n]
                )

            for here in range(line):

                @pl.when(place_ref[1] == here)
                def _():
                    for n in range(line):
                        copy(holder(here, n), n).start()

            for n in range(line):
                copy(0, n).wait()
        piece = half // line
        for n in range(devices):
            start = pl.multiple_of((place_ref[0] ^ n) * block, block)
            for k in range(2):
                rows = [
                    w[pl.ds(start + (2 * m + k) * piece, piece), :] for m in range(line)
                ]
                to = pl.ds((2 * n + k) * half, half)
                w_high[to, :], w_low[to, :] = split(jnp.concatenate(rows, axis=0))

    def step(next_high, next_low, t_high, t_low):
        for n, part in enumerate(parts):
            to = slice(n * half, (n + 1) * half)
            next_high[:, to], next_low[:, to] = split(part[...])
        dot = functools.partial(jnp.dot, preferred_element_type=jnp.float32)
        total = dot(t_low[...], w_high[...])
        total += dot(t_high[...], w_low[...])
        total += dot(t_high[...], w_high[...])
        out_ref[:, :width] = 0.5 * total

    @pl.when(now % 2 == 0)
    def _():
        step(even_high, even_low, odd_high, odd_low)

    @pl.when(now % 2 == 1)
    def _():
        step(odd_high, odd_low, even_high, even_low)


def product(line, place, parts, sources, out, chunk, shape):
    start, width, block, by_line = chunk
    rows, size = parts[0].shape
    depth = size * len(parts)
    tiles = pl.cdiv(rows, ROWS)
    part_spec = pl.BlockSpec((ROWS, size), lambda i, p: (jnp.minimum(i, tiles - 1), 0))
    anywhere = pl.BlockSpec(memory_space=pl.ANY)
    operands = [place, *parts, *sources]
    aliases = {}
    if out is not None:
        aliases = {len(operands): 0}
        operands.append(out)
    others = len(operands) - 1 - len(parts)
    t_half = pltpu.VMEM((ROWS, depth), jnp.bfloat16)
    w_half = pltpu.VMEM((depth, width), jnp.bfloat16)
    return pl.pallas_call(
        functools.partial(product_kernel, line, len(parts) // 2, not by_line),
        grid_spec=pltpu.PrefetchScalarGridSpec(
            num_scalar_prefetch=1,
            grid=(tiles + 1,),
            in_specs=[part_spec] * len(parts) + [anywhere] * others,
            out_specs=pl.BlockSpec(
                (ROWS, block), lambda i, p: (jnp.maximum(i - 1, 0), start // block)
            ),
            scratch_shapes=[
                pltpu.VMEM((depth, width), jnp.float32),
                w_half,
                w_half,
                t_half,
                t_half,
                t_half,
                t_half,
                pltpu.SemaphoreType.DMA((line,)),
            ],
        ),
        out_shape=jax.ShapeDtypeStruct(shape, jnp.float32),
        input_output_aliases=aliases,
        compiler_params=params(),
        cost_estimate=moved(
            4 * (rows * depth + depth * width + rows * width),
            6 * rows * depth * width,
        ),
    )(*operands)


def tie(*values):
    return lax.optimization_barrier(values)


def per_device(line, devices, amplitudes, integrals):
    columns = integrals.shape[1]
    rows = amplitudes.shape[0] // line
    chunks = chunks_of(columns, line)
    outer, inner = [(1, 0), (2, 3)], [(1, 2), (2, 1)]
    both = outer + [(0, 1), (3, 2)]

    def piece(chunk, source):
        return lax.slice_in_dim(source, chunk[0], chunk[0] + chunk[1], axis=1)

    def send(x, pairs):
        return lax.ppermute(x, "ga", pairs)

    def swap(x, mask):
        return lax.ppermute(x, "ka", [(d, d ^ mask) for d in range(devices)])

    near, far = [chunk for chunk in chunks if chunk[3]] or (None, None)
    sources = {}

    turned = []
    for half in range(2):
        blocks = cut(amplitudes.T, line, half)
        blocks = lax.all_to_all(blocks, "ga", split_axis=0, concat_axis=0, tiled=True)
        turned.append(blocks.reshape(-1, rows))
    if near:
        own = piece(near, integrals)
        turned[1], first = tie(turned[1], send(own, both))
    turned[1], integrals = tie(turned[1], integrals)
    if near:
        second = send(piece(near, integrals), inner)

    for chunk in chunks:
        if not chunk[3]:
            sources[chunk] = [lax.all_gather(piece(chunk, integrals), "ga", axis=0, tiled=True)]

    masks = [1 << bit for bit in range(1, devices.bit_length() - 1)]
    held = [{0: turn(half)} for half in turned]
    orders = (masks[::-1], masks)
    across = [{}, {}]
    for level in range(1, len(masks) + 1):
        if level == 2:
            across[0] = {n: swap(block, 1) for n, block in held[0].items()}
            across[1] = {0: swap(held[1][0], 1)}
        if level == 2 and near:
            held, across, first, second = tie(held, across, first, second)
            third, fourth = send(second, outer), send(first, inner)
        elif level > 1:
            held, across = tie(held, across)
        added = [{}, {}]
        for n in range(2, devices, 2):
            if n.bit_count() == level:
                for blocks, new, order in zip(held, added, orders):
                    last = [mask for mask in order if n & mask][-1]
                    new[n] = swap(blocks[n ^ last], last)
        held = [blocks | new for blocks, new in zip(held, added)]
    for blocks, others in zip(held, across):
        for n in sorted(blocks.keys() - others.keys()):
            others[n] = swap(blocks[n], 1)
    parts = [
        (across if n % 2 else held)[half][n - n % 2]
        for n in range(devices)
        for half in range(2)
    ]

    place = jnp.stack([lax.axis_index("ka"), lax.axis_index("ga")])
    if near:
        place, third, fourth = tie(place, third, fourth)
        sources[near] = [own, first, second, third, fourth, send(fourth, outer)]

    out = None
    for n, chunk in enumerate(chunks):
        if near and n == 1:
            out, mine = tie(out, piece(far, integrals))
            first, second = send(mine, both), send(mine, inner)
        elif near and n == 2:
            out, first, second = tie(out, first, second)
            third, fourth = send(second, outer), send(first, inner)
        elif near and n == 3:
            out, third, fourth = tie(out, third, fourth)
            sources[far] = [mine, first, second, third, fourth, send(fourth, outer)]
        out = product(line, place, parts, sources[chunk], out, chunk, (rows, columns))
    return out


def solution(mesh):
    placed = (P(None, ("ka", "ga")), P("ga", "ka"))
    return jax.shard_map(
        functools.partial(per_device, mesh.shape["ga"], mesh.shape["ka"]),
        mesh=mesh,
        in_specs=placed,
        out_specs=P("ga", "ka"),
        check_vma=False,
    )
```

```python
import functools

import jax
import jax.numpy as jnp
from jax import lax
from jax.experimental import pallas as pl
from jax.experimental.pallas import tpu as pltpu
from jax.sharding import PartitionSpec as P

ROWS = 240
WIDE = 512
VMEM_BYTES = 60 * 2**20


def params():
    return pltpu.CompilerParams(vmem_limit_bytes=VMEM_BYTES)


def moved(bytes_accessed, flops=0):
    return pl.CostEstimate(
        flops=flops, bytes_accessed=bytes_accessed, transcendentals=0
    )


def chunks_of(columns):
    if columns == 1920:
        order = [(0, 1024), (1280, 640), (1024, 256)]
        return [(start, width, width) for start, width in order]
    wide = [(n, WIDE, WIDE) for n in range(0, columns - WIDE + 1, WIDE)]
    start = len(wide) * WIDE
    return wide + ([(start, columns - start, WIDE)] if start < columns else [])


def cut_kernel(t_ref, out_ref):
    groups, _, rows = out_ref.shape
    for n in range(groups):
        out_ref[n] = t_ref[:, n * rows : (n + 1) * rows]


def cut(columns, groups, half):
    depth, pairs = columns.shape
    shape = (groups, depth // 2, pairs // groups)
    return pl.pallas_call(
        cut_kernel,
        grid=(1,),
        in_specs=[pl.BlockSpec((depth // 2, pairs), lambda i: (half, 0))],
        out_specs=pl.BlockSpec(shape, lambda i: (0, 0, 0)),
        out_shape=jax.ShapeDtypeStruct(shape, jnp.float32),
        compiler_params=params(),
        cost_estimate=moved(4 * depth * pairs),
    )(columns)


def turn_kernel(t_ref, out_ref):
    out_ref[...] = t_ref[...].T


def turn(columns):
    depth, rows = columns.shape
    width = 512
    return pl.pallas_call(
        turn_kernel,
        grid=(pl.cdiv(rows, width),),
        in_specs=[pl.BlockSpec((depth, width), lambda i: (0, i))],
        out_specs=pl.BlockSpec((width, depth), lambda i: (i, 0)),
        out_shape=jax.ShapeDtypeStruct((rows, depth), jnp.float32),
        compiler_params=params(),
        cost_estimate=moved(8 * depth * rows),
    )(columns)


def split(x):
    high = x.astype(jnp.bfloat16)
    return high, (x - high.astype(jnp.float32)).astype(jnp.bfloat16)


def product_kernel(line, devices, place_ref, *refs):
    parts, w_hbm = refs[: 2 * devices], refs[2 * devices]
    out_ref, w, w_high, w_low, t_high, t_low, arrived = refs[-7:]
    depth, width = w.shape
    block = depth // devices
    half = block // 2

    @pl.when(pl.program_id(0) == 0)
    def _():
        whole = pltpu.make_async_copy(w_hbm, w, arrived)
        whole.start()
        whole.wait()
        piece = half // line
        for n in range(devices):
            start = pl.multiple_of((place_ref[0] ^ n) * block, block)
            for k in range(2):
                rows = [
                    w[pl.ds(start + (2 * m + k) * piece, piece), :] for m in range(line)
                ]
                to = pl.ds((2 * n + k) * half, half)
                w_high[to, :], w_low[to, :] = split(jnp.concatenate(rows, axis=0))

    for n, part in enumerate(parts):
        to = slice(n * half, (n + 1) * half)
        t_high[:, to], t_low[:, to] = split(part[...])
    dot = functools.partial(jnp.dot, preferred_element_type=jnp.float32)
    total = dot(t_low[...], w_high[...])
    total += dot(t_high[...], w_low[...])
    total += dot(t_high[...], w_high[...])
    out_ref[:, :width] = 0.5 * total


def product(line, place, parts, w, out, chunk, full):
    start, width, block = chunk
    rows, size = parts[0].shape
    depth = size * len(parts)
    part_spec = pl.BlockSpec((ROWS, size), lambda i, p: (i, 0))
    anywhere = pl.BlockSpec(memory_space=pl.ANY)
    operands = [place, *parts, w]
    aliases = {}
    if out is not None:
        aliases = {len(operands): 0}
        operands.append(out)
    others = len(operands) - 1 - len(parts)
    t_half = pltpu.VMEM((ROWS, depth), jnp.bfloat16)
    w_half = pltpu.VMEM((depth, width), jnp.bfloat16)
    return pl.pallas_call(
        functools.partial(product_kernel, line, len(parts) // 2),
        grid_spec=pltpu.PrefetchScalarGridSpec(
            num_scalar_prefetch=1,
            grid=(pl.cdiv(rows, ROWS),),
            in_specs=[part_spec] * len(parts) + [anywhere] * others,
            out_specs=pl.BlockSpec((ROWS, block), lambda i, p: (i, start // block)),
            scratch_shapes=[
                pltpu.VMEM((depth, width), jnp.float32),
                w_half,
                w_half,
                t_half,
                t_half,
                pltpu.SemaphoreType.DMA(()),
            ],
        ),
        out_shape=jax.ShapeDtypeStruct((rows, full), jnp.float32),
        input_output_aliases=aliases,
        compiler_params=params(),
        cost_estimate=moved(
            4 * (rows * depth + depth * width + rows * width),
            6 * rows * depth * width,
        ),
    )(*operands)


def tie(*values):
    return lax.optimization_barrier(values)


def per_device(line, devices, amplitudes, integrals):
    columns = integrals.shape[1]
    rows = amplitudes.shape[0] // line
    chunks = chunks_of(columns)

    def swap(x, mask):
        return lax.ppermute(x, "ka", [(d, d ^ mask) for d in range(devices)])

    pieces = [
        lax.slice_in_dim(integrals, start, start + width, axis=1)
        for start, width, _ in chunks
    ]
    pieces[0], amplitudes = tie(pieces[0], amplitudes)
    gathered = [lax.all_gather(x, "ga", axis=0, tiled=True) for x in pieces]

    held = []
    for half in range(2):
        blocks = cut(amplitudes.T, line, half)
        if half:
            blocks, first = tie(blocks, first)
            held.append({0: turn(first)})
        blocks = lax.all_to_all(blocks, "ga", split_axis=0, concat_axis=0, tiled=True)
        first = blocks.reshape(-1, rows)
    held.append({0: turn(first)})

    masks = [1 << bit for bit in range(1, devices.bit_length() - 1)]
    orders = (masks[::-1], masks)
    across = [{}, {}]
    for level in range(1, len(masks) + 1):
        if level == 2:
            across[0] = {n: swap(block, 1) for n, block in held[0].items()}
            across[1] = {0: swap(held[1][0], 1)}
        if level > 1:
            held, across = tie(held, across)
        added = [{}, {}]
        for n in range(2, devices, 2):
            if n.bit_count() == level:
                for blocks, new, order in zip(held, added, orders):
                    last = [mask for mask in order if n & mask][-1]
                    new[n] = swap(blocks[n ^ last], last)
        held = [blocks | new for blocks, new in zip(held, added)]
    for blocks, others in zip(held, across):
        for n in sorted(blocks.keys() - others.keys()):
            others[n] = swap(blocks[n], 1)
    parts = [
        (across if n % 2 else held)[half][n - n % 2]
        for n in range(devices)
        for half in range(2)
    ]

    place = lax.axis_index("ka").astype(jnp.int32).reshape(1)
    out = None
    for chunk, w in zip(chunks, gathered):
        out = product(line, place, parts, w, out, chunk, columns)
    return out


def solution(mesh):
    placed = (P(None, ("ka", "ga")), P("ga", "ka"))
    return jax.shard_map(
        functools.partial(per_device, mesh.shape["ga"], mesh.shape["ka"]),
        mesh=mesh,
        in_specs=placed,
        out_specs=P("ga", "ka"),
        check_vma=False,
    )
```

```python
import functools

import jax
import jax.numpy as jnp
from jax import lax
from jax.experimental import pallas as pl
from jax.experimental.pallas import tpu as pltpu
from jax.sharding import PartitionSpec as P

ROWS = 240
WIDE = 512
VMEM_BYTES = 60 * 2**20


def params():
    return pltpu.CompilerParams(vmem_limit_bytes=VMEM_BYTES)


def moved(bytes_accessed, flops=0):
    return pl.CostEstimate(
        flops=flops, bytes_accessed=bytes_accessed, transcendentals=0
    )


def chunks_of(columns):
    if columns == 1920:
        order = [(0, 1024), (1280, 640), (1024, 256)]
        return [(start, width, width) for start, width in order]
    wide = [(n, WIDE, WIDE) for n in range(0, columns - WIDE + 1, WIDE)]
    start = len(wide) * WIDE
    return wide + ([(start, columns - start, WIDE)] if start < columns else [])


def cut_kernel(t_ref, out_ref):
    groups, _, rows = out_ref.shape
    for n in range(groups):
        out_ref[n] = t_ref[:, n * rows : (n + 1) * rows]


def cut(columns, groups, half):
    depth, pairs = columns.shape
    shape = (groups, depth // 2, pairs // groups)
    return pl.pallas_call(
        cut_kernel,
        grid=(1,),
        in_specs=[pl.BlockSpec((depth // 2, pairs), lambda i: (half, 0))],
        out_specs=pl.BlockSpec(shape, lambda i: (0, 0, 0)),
        out_shape=jax.ShapeDtypeStruct(shape, jnp.float32),
        compiler_params=params(),
        cost_estimate=moved(4 * depth * pairs),
    )(columns)


def turn_kernel(t_ref, out_ref):
    out_ref[...] = t_ref[...].T


def turn(columns):
    depth, rows = columns.shape
    width = 512
    return pl.pallas_call(
        turn_kernel,
        grid=(pl.cdiv(rows, width),),
        in_specs=[pl.BlockSpec((depth, width), lambda i: (0, i))],
        out_specs=pl.BlockSpec((width, depth), lambda i: (i, 0)),
        out_shape=jax.ShapeDtypeStruct((rows, depth), jnp.float32),
        compiler_params=params(),
        cost_estimate=moved(8 * depth * rows),
    )(columns)


def split(x):
    high = x.astype(jnp.bfloat16)
    return high, (x - high.astype(jnp.float32)).astype(jnp.bfloat16)


def product_kernel(line, devices, given, place_ref, *refs):
    parts, w_hbm = refs[:given], refs[given]
    if given == 2:
        t_high, t_low = parts
        out_ref, w, w_high, w_low, arrived = refs[-5:]
    else:
        out_ref, t_high, t_low, w, w_high, w_low, arrived = refs[-7:]
    depth, width = w.shape
    block = depth // devices
    half = block // 2

    @pl.when(pl.program_id(0) == 0)
    def _():
        whole = pltpu.make_async_copy(w_hbm, w, arrived)
        whole.start()
        whole.wait()
        piece = half // line
        for n in range(devices):
            start = pl.multiple_of((place_ref[0] ^ n) * block, block)
            for k in range(2):
                rows = [
                    w[pl.ds(start + (2 * m + k) * piece, piece), :] for m in range(line)
                ]
                to = pl.ds((2 * n + k) * half, half)
                w_high[to, :], w_low[to, :] = split(jnp.concatenate(rows, axis=0))

    if given > 2:
        for n, part in enumerate(parts):
            to = slice(n * half, (n + 1) * half)
            t_high[:, to], t_low[:, to] = split(part[...])
    dot = functools.partial(jnp.dot, preferred_element_type=jnp.float32)
    total = dot(t_low[...], w_high[...])
    total += dot(t_high[...], w_low[...])
    total += dot(t_high[...], w_high[...])
    out_ref[:, :width] = 0.5 * total


def product(line, devices, place, parts, w, out, chunk, full):
    start, width, block = chunk
    rows, size = parts[0].shape
    given = len(parts)
    depth = w.shape[0]
    t_spec = pl.BlockSpec((ROWS, depth), lambda i, p: (i, 0))
    part_spec = pl.BlockSpec((ROWS, size), lambda i, p: (i, 0))
    out_spec = pl.BlockSpec((ROWS, block), lambda i, p: (i, start // block))
    out_shape = jax.ShapeDtypeStruct((rows, full), jnp.float32)
    t_shape = jax.ShapeDtypeStruct((rows, depth), jnp.bfloat16)
    anywhere = pl.BlockSpec(memory_space=pl.ANY)
    operands = [place, *parts, w]
    aliases = {}
    if out is not None:
        aliases = {len(operands): 0}
        operands.append(out)
    w_half = pltpu.VMEM((depth, width), jnp.bfloat16)
    return pl.pallas_call(
        functools.partial(product_kernel, line, devices, given),
        grid_spec=pltpu.PrefetchScalarGridSpec(
            num_scalar_prefetch=1,
            grid=(pl.cdiv(rows, ROWS),),
            in_specs=[part_spec] * given + [anywhere] * (len(operands) - 1 - given),
            out_specs=[out_spec] + [t_spec] * (2 if given > 2 else 0),
            scratch_shapes=[
                pltpu.VMEM((depth, width), jnp.float32),
                w_half,
                w_half,
                pltpu.SemaphoreType.DMA(()),
            ],
        ),
        out_shape=[out_shape] + [t_shape] * (2 if given > 2 else 0),
        input_output_aliases=aliases,
        compiler_params=params(),
        cost_estimate=moved(
            4 * (rows * depth + depth * width + rows * width),
            6 * rows * depth * width,
        ),
    )(*operands)


def tie(*values):
    return lax.optimization_barrier(values)


def per_device(line, devices, amplitudes, integrals):
    columns = integrals.shape[1]
    rows = amplitudes.shape[0] // line
    chunks = chunks_of(columns)

    def swap(x, mask):
        return lax.ppermute(x, "ka", [(d, d ^ mask) for d in range(devices)])

    held = []
    for half in range(2):
        blocks = cut(amplitudes.T, line, half)
        if half:
            blocks, first, integrals = tie(blocks, first, integrals)
            held.append({0: turn(first)})
        blocks = lax.all_to_all(blocks, "ga", split_axis=0, concat_axis=0, tiled=True)
        first = blocks.reshape(-1, rows)
    held.append({0: turn(first)})

    pieces = [
        lax.slice_in_dim(integrals, start, start + width, axis=1)
        for start, width, _ in chunks
    ]
    gathered = [lax.all_gather(x, "ga", axis=0, tiled=True) for x in pieces]

    masks = [1 << bit for bit in range(1, devices.bit_length() - 1)]
    orders = (masks[::-1], masks)
    across = [{}, {}]
    for level in range(1, len(masks) + 1):
        if level == 2:
            across[0] = {n: swap(block, 1) for n, block in held[0].items()}
            across[1] = {0: swap(held[1][0], 1)}
        if level > 1:
            held, across = tie(held, across)
        added = [{}, {}]
        for n in range(2, devices, 2):
            if n.bit_count() == level:
                for blocks, new, order in zip(held, added, orders):
                    last = [mask for mask in order if n & mask][-1]
                    new[n] = swap(blocks[n ^ last], last)
        held = [blocks | new for blocks, new in zip(held, added)]
    for blocks, others in zip(held, across):
        for n in sorted(blocks.keys() - others.keys()):
            others[n] = swap(blocks[n], 1)
    parts = [
        (across if n % 2 else held)[half][n - n % 2]
        for n in range(devices)
        for half in range(2)
    ]

    place = lax.axis_index("ka").astype(jnp.int32).reshape(1)
    out = None
    for chunk, w in zip(chunks, gathered):
        out, *halves = product(line, devices, place, parts, w, out, chunk, columns)
        parts = halves or parts
    return out


def solution(mesh):
    placed = (P(None, ("ka", "ga")), P("ga", "ka"))
    return jax.shard_map(
        functools.partial(per_device, mesh.shape["ga"], mesh.shape["ka"]),
        mesh=mesh,
        in_specs=placed,
        out_specs=P("ga", "ka"),
        check_vma=False,
    )
```

```python
import functools

import jax
import jax.numpy as jnp
from jax import lax
from jax.experimental import pallas as pl
from jax.experimental.pallas import tpu as pltpu
from jax.sharding import PartitionSpec as P

ROWS = 240
WIDE = 512
VMEM_BYTES = 60 * 2**20


def params():
    return pltpu.CompilerParams(vmem_limit_bytes=VMEM_BYTES)


def moved(bytes_accessed, flops=0):
    return pl.CostEstimate(
        flops=flops, bytes_accessed=bytes_accessed, transcendentals=0
    )


def chunks_of(columns):
    if columns == 1920:
        order = [(0, 1024), (1280, 640), (1024, 256)]
        return [(start, width, width) for start, width in order]
    wide = [(n, WIDE, WIDE) for n in range(0, columns - WIDE + 1, WIDE)]
    start = len(wide) * WIDE
    return wide + ([(start, columns - start, WIDE)] if start < columns else [])


def cut_kernel(t_ref, out_ref):
    groups, _, rows = out_ref.shape
    for n in range(groups):
        out_ref[n] = t_ref[:, n * rows : (n + 1) * rows]


def cut(columns, groups, half):
    depth, pairs = columns.shape
    shape = (groups, depth // 2, pairs // groups)
    return pl.pallas_call(
        cut_kernel,
        grid=(1,),
        in_specs=[pl.BlockSpec((depth // 2, pairs), lambda i: (half, 0))],
        out_specs=pl.BlockSpec(shape, lambda i: (0, 0, 0)),
        out_shape=jax.ShapeDtypeStruct(shape, jnp.float32),
        compiler_params=params(),
        cost_estimate=moved(4 * depth * pairs),
    )(columns)


def turn_kernel(t_ref, out_ref):
    out_ref[...] = t_ref[...].T


def turn(columns):
    depth, rows = columns.shape
    width = 512
    return pl.pallas_call(
        turn_kernel,
        grid=(pl.cdiv(rows, width),),
        in_specs=[pl.BlockSpec((depth, width), lambda i: (0, i))],
        out_specs=pl.BlockSpec((width, depth), lambda i: (i, 0)),
        out_shape=jax.ShapeDtypeStruct((rows, depth), jnp.float32),
        compiler_params=params(),
        cost_estimate=moved(8 * depth * rows),
    )(columns)


def split(x):
    high = x.astype(jnp.bfloat16)
    return high, (x - high.astype(jnp.float32)).astype(jnp.bfloat16)


def product_kernel(devices, place_ref, *refs):
    parts, w_hbm = refs[: 2 * devices], refs[2 * devices]
    out_ref, t_ref, w, w_high, w_low, t_high, t_low, arrived = refs[-8:]
    depth, width = w.shape
    block = depth // devices

    @pl.when(pl.program_id(0) == 0)
    def _():
        whole = pltpu.make_async_copy(w_hbm, w, arrived)
        whole.start()
        whole.wait()
        for n in range(devices):
            rows = slice(n * block, (n + 1) * block)
            w_high[rows, :], w_low[rows, :] = split(w[rows, :])

    for n in range(devices):
        value = jnp.concatenate([parts[2 * n][...], parts[2 * n + 1][...]], axis=1)
        to = pl.ds(pl.multiple_of((place_ref[0] ^ n) * block, block), block)
        t_ref[:, to] = value
        t_high[:, to], t_low[:, to] = split(value)
    dot = functools.partial(jnp.dot, preferred_element_type=jnp.float32)
    total = dot(t_low[...], w_high[...])
    total += dot(t_high[...], w_low[...])
    total += dot(t_high[...], w_high[...])
    out_ref[:, :width] = 0.5 * total


def product(place, parts, w, chunk, full):
    start, width, block = chunk
    rows, size = parts[0].shape
    depth = w.shape[0]
    t_half = pltpu.VMEM((ROWS, depth), jnp.bfloat16)
    w_half = pltpu.VMEM((depth, width), jnp.bfloat16)
    return pl.pallas_call(
        functools.partial(product_kernel, len(parts) // 2),
        grid_spec=pltpu.PrefetchScalarGridSpec(
            num_scalar_prefetch=1,
            grid=(pl.cdiv(rows, ROWS),),
            in_specs=[pl.BlockSpec((ROWS, size), lambda i, p: (i, 0))] * len(parts)
            + [pl.BlockSpec(memory_space=pl.ANY)],
            out_specs=[
                pl.BlockSpec((ROWS, block), lambda i, p: (i, start // block)),
                pl.BlockSpec((ROWS, depth), lambda i, p: (i, 0)),
            ],
            scratch_shapes=[
                pltpu.VMEM((depth, width), jnp.float32),
                w_half,
                w_half,
                t_half,
                t_half,
                pltpu.SemaphoreType.DMA(()),
            ],
        ),
        out_shape=[
            jax.ShapeDtypeStruct((rows, full), jnp.float32),
            jax.ShapeDtypeStruct((rows, depth), jnp.float32),
        ],
        compiler_params=params(),
        cost_estimate=moved(
            4 * (2 * rows * depth + depth * width + rows * width),
            6 * rows * depth * width,
        ),
    )(place, *parts, w)


def tie(*values):
    return lax.optimization_barrier(values)


def per_device(line, devices, amplitudes, integrals):
    columns = integrals.shape[1]
    rows = amplitudes.shape[0] // line
    chunks = chunks_of(columns)

    def swap(x, mask):
        return lax.ppermute(x, "ka", [(d, d ^ mask) for d in range(devices)])

    def gather(n, source):
        start, width, _ = chunks[n]
        x = lax.slice_in_dim(source, start, start + width, axis=1)
        x = x.reshape(devices // line, line, 2, -1, width).swapaxes(1, 2)
        return lax.all_gather(x.reshape(-1, width), "ga", axis=0, tiled=True)

    source, amplitudes = tie(integrals, amplitudes)
    gathered = [gather(0, source)]

    held = []
    for half in range(2):
        blocks = cut(amplitudes.T, line, half)
        if half:
            blocks, first, source = tie(blocks, first, integrals)
            gathered.append(gather(1, source))
            held.append({0: turn(first)})
        blocks = lax.all_to_all(blocks, "ga", split_axis=0, concat_axis=0, tiled=True)
        first = blocks.reshape(-1, rows)
    held.append({0: turn(first)})

    masks = [1 << bit for bit in range(1, devices.bit_length() - 1)]
    orders = (masks[::-1], masks)
    across = [{}, {}]
    for half, order in enumerate(orders):
        blocks = held[half]
        if half:
            across[1] = {0: swap(blocks[0], 1)}
        for level in range(1, len(masks) + 1):
            if half and level == 2:
                held, across, source = tie(held, across, integrals)
                gathered += [gather(n, source) for n in range(2, len(chunks))]
                blocks = held[1]
            if half and level == 2 == len(masks):
                some = rows // 16 * 8
                by_first = swap(blocks[masks[0]][:some], masks[1])
                by_second = swap(blocks[masks[1]][some:], masks[0])
                blocks[masks[0] | masks[1]] = jnp.concatenate([by_first, by_second])
                continue
            for n in range(2, devices, 2):
                if n.bit_count() == level:
                    last = [mask for mask in order if n & mask][-1]
                    blocks[n] = swap(blocks[n ^ last], last)
        for n in sorted(blocks.keys() - across[half].keys()):
            across[half][n] = swap(blocks[n], 1)
    parts = [
        (across if n % 2 else held)[half][n - n % 2]
        for n in range(devices)
        for half in range(2)
    ]

    place = lax.axis_index("ka").astype(jnp.int32)
    out, whole = product(place.reshape(1), parts, gathered[0], chunks[0], columns)
    for (start, _, _), w in zip(chunks[1:], gathered[1:]):
        ladder = jnp.dot(
            whole,
            w,
            precision=lax.Precision.HIGH,
            preferred_element_type=jnp.float32,
        )
        out = lax.dynamic_update_slice_in_dim(out, 0.5 * ladder, start, axis=1)
    return out


def solution(mesh):
    placed = (P(None, ("ka", "ga")), P("ga", "ka"))
    return jax.shard_map(
        functools.partial(per_device, mesh.shape["ga"], mesh.shape["ka"]),
        mesh=mesh,
        in_specs=placed,
        out_specs=P("ga", "ka"),
        check_vma=False,
    )
```

```python
import functools

import jax
import jax.numpy as jnp
from jax import lax
from jax.experimental import pallas as pl
from jax.experimental.pallas import tpu as pltpu
from jax.sharding import PartitionSpec as P

ROWS = 240
WIDE = 512
VMEM_BYTES = 60 * 2**20


def params():
    return pltpu.CompilerParams(vmem_limit_bytes=VMEM_BYTES)


def moved(bytes_accessed, flops=0):
    return pl.CostEstimate(
        flops=flops, bytes_accessed=bytes_accessed, transcendentals=0
    )


def chunks_of(columns):
    if columns == 1920:
        order = [(0, 1024), (1280, 640), (1024, 256)]
        return [(start, width, width) for start, width in order]
    wide = [(n, WIDE, WIDE) for n in range(0, columns - WIDE + 1, WIDE)]
    start = len(wide) * WIDE
    return wide + ([(start, columns - start, WIDE)] if start < columns else [])


def cut_kernel(t_ref, out_ref):
    groups, _, rows = out_ref.shape
    for n in range(groups):
        out_ref[n] = t_ref[:, n * rows : (n + 1) * rows]


def cut(columns, groups, half):
    depth, pairs = columns.shape
    shape = (groups, depth // 2, pairs // groups)
    return pl.pallas_call(
        cut_kernel,
        grid=(1,),
        in_specs=[pl.BlockSpec((depth // 2, pairs), lambda i: (half, 0))],
        out_specs=pl.BlockSpec(shape, lambda i: (0, 0, 0)),
        out_shape=jax.ShapeDtypeStruct(shape, jnp.float32),
        compiler_params=params(),
        cost_estimate=moved(4 * depth * pairs),
    )(columns)


def turn_kernel(t_ref, out_ref):
    out_ref[...] = t_ref[...].T


def turn(columns):
    depth, rows = columns.shape
    width = 512
    return pl.pallas_call(
        turn_kernel,
        grid=(pl.cdiv(rows, width),),
        in_specs=[pl.BlockSpec((depth, width), lambda i: (0, i))],
        out_specs=pl.BlockSpec((width, depth), lambda i: (i, 0)),
        out_shape=jax.ShapeDtypeStruct((rows, depth), jnp.float32),
        compiler_params=params(),
        cost_estimate=moved(8 * depth * rows),
    )(columns)


def split(x):
    high = x.astype(jnp.bfloat16)
    return high, (x - high.astype(jnp.float32)).astype(jnp.bfloat16)


def product_kernel(devices, place_ref, *refs):
    parts, w_hbm = refs[: 2 * devices], refs[2 * devices]
    out_ref, t_high, t_low, w, w_high, w_low, arrived = refs[-7:]
    depth, width = w.shape
    block = depth // devices

    @pl.when(pl.program_id(0) == 0)
    def _():
        whole = pltpu.make_async_copy(w_hbm, w, arrived)
        whole.start()
        whole.wait()
        for n in range(devices):
            rows = slice(n * block, (n + 1) * block)
            w_high[rows, :], w_low[rows, :] = split(w[rows, :])

    for n in range(devices):
        value = jnp.concatenate([parts[2 * n][...], parts[2 * n + 1][...]], axis=1)
        to = pl.ds(pl.multiple_of((place_ref[0] ^ n) * block, block), block)
        t_high[:, to], t_low[:, to] = split(value)
    dot = functools.partial(jnp.dot, preferred_element_type=jnp.float32)
    total = dot(t_low[...], w_high[...])
    total += dot(t_high[...], w_low[...])
    total += dot(t_high[...], w_high[...])
    out_ref[:, :width] = 0.5 * total


def product(place, parts, w, chunk, full):
    start, width, block = chunk
    rows, size = parts[0].shape
    depth = w.shape[0]
    w_half = pltpu.VMEM((depth, width), jnp.bfloat16)
    return pl.pallas_call(
        functools.partial(product_kernel, len(parts) // 2),
        grid_spec=pltpu.PrefetchScalarGridSpec(
            num_scalar_prefetch=1,
            grid=(pl.cdiv(rows, ROWS),),
            in_specs=[pl.BlockSpec((ROWS, size), lambda i, p: (i, 0))] * len(parts)
            + [pl.BlockSpec(memory_space=pl.ANY)],
            out_specs=[
                pl.BlockSpec((ROWS, block), lambda i, p: (i, start // block)),
                pl.BlockSpec((ROWS, depth), lambda i, p: (i, 0)),
                pl.BlockSpec((ROWS, depth), lambda i, p: (i, 0)),
            ],
            scratch_shapes=[
                pltpu.VMEM((depth, width), jnp.float32),
                w_half,
                w_half,
                pltpu.SemaphoreType.DMA(()),
            ],
        ),
        out_shape=[
            jax.ShapeDtypeStruct((rows, full), jnp.float32),
            jax.ShapeDtypeStruct((rows, depth), jnp.bfloat16),
            jax.ShapeDtypeStruct((rows, depth), jnp.bfloat16),
        ],
        compiler_params=params(),
        cost_estimate=moved(
            4 * (2 * rows * depth + depth * width + rows * width),
            6 * rows * depth * width,
        ),
    )(place, *parts, w)


def tie(*values):
    return lax.optimization_barrier(values)


def per_device(line, devices, amplitudes, integrals):
    columns = integrals.shape[1]
    rows = amplitudes.shape[0] // line
    chunks = chunks_of(columns)

    def swap(x, mask):
        return lax.ppermute(x, "ka", [(d, d ^ mask) for d in range(devices)])

    def gather(n, source):
        start, width, _ = chunks[n]
        x = lax.slice_in_dim(source, start, start + width, axis=1)
        x = x.reshape(devices // line, line, 2, -1, width).swapaxes(1, 2)
        return lax.all_gather(x.reshape(-1, width), "ga", axis=0, tiled=True)

    source, amplitudes = tie(integrals, amplitudes)
    gathered = [gather(0, source)]

    held = []
    for half in range(2):
        blocks = cut(amplitudes.T, line, half)
        if half:
            blocks, first, source = tie(blocks, first, integrals)
            gathered.append(gather(1, source))
            held.append({0: turn(first)})
        blocks = lax.all_to_all(blocks, "ga", split_axis=0, concat_axis=0, tiled=True)
        first = blocks.reshape(-1, rows)
    held.append({0: turn(first)})

    masks = [1 << bit for bit in range(1, devices.bit_length() - 1)]
    orders = (masks[::-1], masks)
    across = [{}, {}]
    for half, order in enumerate(orders):
        blocks = held[half]
        if half:
            across[1] = {0: swap(blocks[0], 1)}
        for level in range(1, len(masks) + 1):
            if half and level == 2:
                held, across, source = tie(held, across, integrals)
                gathered += [gather(n, source) for n in range(2, len(chunks))]
                blocks = held[1]
            if half and level == 2 == len(masks):
                some = rows // 16 * 8
                by_first = swap(blocks[masks[0]][:some], masks[1])
                by_second = swap(blocks[masks[1]][some:], masks[0])
                blocks[masks[0] | masks[1]] = jnp.concatenate([by_first, by_second])
                continue
            for n in range(2, devices, 2):
                if n.bit_count() == level:
                    last = [mask for mask in order if n & mask][-1]
                    blocks[n] = swap(blocks[n ^ last], last)
        for n in sorted(blocks.keys() - across[half].keys()):
            across[half][n] = swap(blocks[n], 1)
    parts = [
        (across if n % 2 else held)[half][n - n % 2]
        for n in range(devices)
        for half in range(2)
    ]

    place = lax.axis_index("ka").astype(jnp.int32)
    out, *t = product(place.reshape(1), parts, gathered[0], chunks[0], columns)
    dot = functools.partial(jnp.dot, preferred_element_type=jnp.float32)
    for (start, width, _), w in zip(chunks[1:], gathered[1:]):
        out, (t_high, t_low), w = tie(out, t, w)
        high = lax.reduce_precision(w, exponent_bits=8, mantissa_bits=7)
        w_low = (w - high).astype(jnp.bfloat16)
        w_high = high.astype(jnp.bfloat16)
        both = dot(t_high, jnp.concatenate([w_low, w_high], axis=1))
        ladder = dot(t_low, w_high) + both[:, :width] + both[:, width:]
        out = lax.dynamic_update_slice_in_dim(out, 0.5 * ladder, start, axis=1)
    return out


def solution(mesh):
    placed = (P(None, ("ka", "ga")), P("ga", "ka"))
    return jax.shard_map(
        functools.partial(per_device, mesh.shape["ga"], mesh.shape["ka"]),
        mesh=mesh,
        in_specs=placed,
        out_specs=P("ga", "ka"),
        check_vma=False,
    )
```

```python
import functools

import jax
import jax.numpy as jnp
from jax import lax
from jax.experimental import pallas as pl
from jax.experimental.pallas import tpu as pltpu
from jax.sharding import PartitionSpec as P

ROWS = 240
WIDE = 512
VMEM_BYTES = 60 * 2**20


def params():
    return pltpu.CompilerParams(vmem_limit_bytes=VMEM_BYTES)


def moved(bytes_accessed, flops=0):
    return pl.CostEstimate(
        flops=flops, bytes_accessed=bytes_accessed, transcendentals=0
    )


def chunks_of(columns, line):
    if columns == 1920 and line == 4:
        order = [(0, 896), (896, 512), (1408, 256), (1664, 256)]
        *gathered, ringed = [(start, width, width) for start, width in order]
        return gathered, ringed
    wide = [(n, WIDE, WIDE) for n in range(0, columns - WIDE + 1, WIDE)]
    start = len(wide) * WIDE
    rest = [(start, columns - start, WIDE)] if start < columns else []
    return wide + rest, None


def cut_kernel(t_ref, out_ref):
    groups, _, rows = out_ref.shape
    for n in range(groups):
        out_ref[n] = t_ref[:, n * rows : (n + 1) * rows]


def cut(columns, groups, half):
    depth, pairs = columns.shape
    shape = (groups, depth // 2, pairs // groups)
    return pl.pallas_call(
        cut_kernel,
        grid=(1,),
        in_specs=[pl.BlockSpec((depth // 2, pairs), lambda i: (half, 0))],
        out_specs=pl.BlockSpec(shape, lambda i: (0, 0, 0)),
        out_shape=jax.ShapeDtypeStruct(shape, jnp.float32),
        compiler_params=params(),
        cost_estimate=moved(4 * depth * pairs),
    )(columns)


def turn_kernel(t_ref, out_ref):
    out_ref[...] = t_ref[...].T


def turn(columns):
    depth, rows = columns.shape
    width = 512
    return pl.pallas_call(
        turn_kernel,
        grid=(pl.cdiv(rows, width),),
        in_specs=[pl.BlockSpec((depth, width), lambda i: (0, i))],
        out_specs=pl.BlockSpec((width, depth), lambda i: (i, 0)),
        out_shape=jax.ShapeDtypeStruct((rows, depth), jnp.float32),
        compiler_params=params(),
        cost_estimate=moved(8 * depth * rows),
    )(columns)


def split(x):
    high = x.astype(jnp.bfloat16)
    return high, (x - high.astype(jnp.float32)).astype(jnp.bfloat16)


def product_kernel(devices, place_ref, *refs):
    parts, w_hbm = refs[: 2 * devices], refs[2 * devices]
    out_ref, t_ref, w, w_high, w_low, t_high, t_low, arrived = refs[-8:]
    depth, width = w.shape
    block = depth // devices

    @pl.when(pl.program_id(0) == 0)
    def _():
        whole = pltpu.make_async_copy(w_hbm, w, arrived)
        whole.start()
        whole.wait()
        for n in range(devices):
            rows = slice(n * block, (n + 1) * block)
            w_high[rows, :], w_low[rows, :] = split(w[rows, :])

    for n in range(devices):
        value = jnp.concatenate([parts[2 * n][...], parts[2 * n + 1][...]], axis=1)
        to = pl.ds(pl.multiple_of((place_ref[0] ^ n) * block, block), block)
        t_ref[:, to] = value
        t_high[:, to], t_low[:, to] = split(value)
    dot = functools.partial(jnp.dot, preferred_element_type=jnp.float32)
    total = dot(t_low[...], w_high[...])
    total += dot(t_high[...], w_low[...])
    total += dot(t_high[...], w_high[...])
    out_ref[:, :width] = 0.5 * total


def product(place, parts, w, chunk, full):
    start, width, block = chunk
    rows, size = parts[0].shape
    depth = w.shape[0]
    t_half = pltpu.VMEM((ROWS, depth), jnp.bfloat16)
    w_half = pltpu.VMEM((depth, width), jnp.bfloat16)
    return pl.pallas_call(
        functools.partial(product_kernel, len(parts) // 2),
        grid_spec=pltpu.PrefetchScalarGridSpec(
            num_scalar_prefetch=1,
            grid=(pl.cdiv(rows, ROWS),),
            in_specs=[pl.BlockSpec((ROWS, size), lambda i, p: (i, 0))] * len(parts)
            + [pl.BlockSpec(memory_space=pl.ANY)],
            out_specs=[
                pl.BlockSpec((ROWS, block), lambda i, p: (i, start // block)),
                pl.BlockSpec((ROWS, depth), lambda i, p: (i, 0)),
            ],
            scratch_shapes=[
                pltpu.VMEM((depth, width), jnp.float32),
                w_half,
                w_half,
                t_half,
                t_half,
                pltpu.SemaphoreType.DMA(()),
            ],
        ),
        out_shape=[
            jax.ShapeDtypeStruct((rows, full), jnp.float32),
            jax.ShapeDtypeStruct((rows, depth), jnp.float32),
        ],
        compiler_params=params(),
        cost_estimate=moved(
            4 * (2 * rows * depth + depth * width + rows * width),
            6 * rows * depth * width,
        ),
    )(place, *parts, w)


def tie(*values):
    return lax.optimization_barrier(values)


def per_device(line, devices, amplitudes, integrals):
    columns = integrals.shape[1]
    rows = amplitudes.shape[0] // line
    chunks, ringed = chunks_of(columns, line)

    def swap(x, mask):
        return lax.ppermute(x, "ka", [(d, d ^ mask) for d in range(devices)])

    def piece(chunk, source):
        start, width, _ = chunk
        x = lax.slice_in_dim(source, start, start + width, axis=1)
        x = x.reshape(devices // line, line, 2, -1, width).swapaxes(1, 2)
        return x.reshape(-1, width)

    def gather(n, source):
        return lax.all_gather(piece(chunks[n], source), "ga", axis=0, tiled=True)

    def forward(x):
        return lax.ppermute(x, "ga", [(n, (n + 1) % line) for n in range(line)])

    gathered = []
    ring = []
    if ringed:
        own, amplitudes = tie(piece(ringed, integrals), amplitudes)
        ring = [own, forward(own)]

    held = []
    for half in range(2):
        blocks = cut(amplitudes.T, line, half)
        if half:
            blocks, first, ring, source = tie(blocks, first, ring, integrals)
            gathered.append(gather(0, source))
            if ringed:
                ring.append(forward(ring[-1]))
            held.append({0: turn(first)})
        blocks = lax.all_to_all(blocks, "ga", split_axis=0, concat_axis=0, tiled=True)
        first = blocks.reshape(-1, rows)
    first, ring = tie(first, ring)
    held.append({0: turn(first)})

    masks = [1 << bit for bit in range(1, devices.bit_length() - 1)]
    orders = (masks[::-1], masks)
    across = [{}, {}]
    for half, order in enumerate(orders):
        blocks = held[half]
        if half:
            across[1] = {0: swap(blocks[0], 1)}
        for level in range(1, len(masks) + 1):
            if half and level == 2:
                held, across, ring, source = tie(held, across, ring, integrals)
                gathered += [gather(n, source) for n in range(1, len(chunks))]
                blocks = held[1]
            if half and level == 2 == len(masks):
                some = rows // 16 * 8
                by_first = swap(blocks[masks[0]][:some], masks[1])
                by_second = swap(blocks[masks[1]][some:], masks[0])
                blocks[masks[0] | masks[1]] = jnp.concatenate([by_first, by_second])
                continue
            for n in range(2, devices, 2):
                if n.bit_count() == level:
                    last = [mask for mask in order if n & mask][-1]
                    blocks[n] = swap(blocks[n ^ last], last)
        for n in sorted(blocks.keys() - across[half].keys()):
            across[half][n] = swap(blocks[n], 1)
    parts = [
        (across if n % 2 else held)[half][n - n % 2]
        for n in range(devices)
        for half in range(2)
    ]

    place = lax.axis_index("ka").astype(jnp.int32)
    if ringed:
        place, ring, parts = tie(place, ring, parts)
        ring.append(forward(ring[-1]))
    out, whole = product(place.reshape(1), parts, gathered[0], chunks[0], columns)

    def rest(out, chunk, w):
        ladder = jnp.dot(
            whole, w, precision=lax.Precision.HIGH, preferred_element_type=jnp.float32
        )
        return lax.dynamic_update_slice_in_dim(out, 0.5 * ladder, chunk[0], axis=1)

    if ringed:
        here = lax.axis_index("ga").astype(jnp.uint32)
        size = own.shape[0]
        w = jnp.zeros((line * size, ringed[1]), jnp.float32)
        for n, shard in enumerate(ring):
            row = lax.rem(here + jnp.uint32(line - n), jnp.uint32(line))
            row = row * jnp.uint32(size)
            w = lax.dynamic_update_slice(w, shard, (row, jnp.uint32(0)))
        out = rest(out, ringed, w)
    for chunk, w in zip(chunks[1:], gathered[1:]):
        out = rest(out, chunk, w)
    return out


def solution(mesh):
    placed = (P(None, ("ka", "ga")), P("ga", "ka"))
    return jax.shard_map(
        functools.partial(per_device, mesh.shape["ga"], mesh.shape["ka"]),
        mesh=mesh,
        in_specs=placed,
        out_specs=P("ga", "ka"),
        check_vma=False,
    )
```

```python
import functools

import jax
import jax.numpy as jnp
from jax import lax
from jax.experimental import pallas as pl
from jax.experimental.pallas import tpu as pltpu
from jax.sharding import PartitionSpec as P

ROWS = 240
WIDE = 512
VMEM_BYTES = 60 * 2**20


def params():
    return pltpu.CompilerParams(vmem_limit_bytes=VMEM_BYTES)


def moved(bytes_accessed, flops=0):
    return pl.CostEstimate(
        flops=flops, bytes_accessed=bytes_accessed, transcendentals=0
    )


def chunks_of(columns):
    if columns == 1920:
        order = [(0, 1024), (1280, 640), (1024, 256)]
        return [(start, width, width) for start, width in order]
    wide = [(n, WIDE, WIDE) for n in range(0, columns - WIDE + 1, WIDE)]
    start = len(wide) * WIDE
    return wide + ([(start, columns - start, WIDE)] if start < columns else [])


def cut_kernel(t_ref, out_ref):
    groups, _, rows = out_ref.shape
    for n in range(groups):
        out_ref[n] = t_ref[:, n * rows : (n + 1) * rows]


def cut(columns, groups, half):
    depth, pairs = columns.shape
    shape = (groups, depth // 2, pairs // groups)
    return pl.pallas_call(
        cut_kernel,
        grid=(1,),
        in_specs=[pl.BlockSpec((depth // 2, pairs), lambda i: (half, 0))],
        out_specs=pl.BlockSpec(shape, lambda i: (0, 0, 0)),
        out_shape=jax.ShapeDtypeStruct(shape, jnp.float32),
        compiler_params=params(),
        cost_estimate=moved(4 * depth * pairs),
    )(columns)


def turn_kernel(t_ref, out_ref):
    out_ref[...] = t_ref[...].T


def turn(columns):
    depth, rows = columns.shape
    width = 512
    return pl.pallas_call(
        turn_kernel,
        grid=(pl.cdiv(rows, width),),
        in_specs=[pl.BlockSpec((depth, width), lambda i: (0, i))],
        out_specs=pl.BlockSpec((width, depth), lambda i: (i, 0)),
        out_shape=jax.ShapeDtypeStruct((rows, depth), jnp.float32),
        compiler_params=params(),
        cost_estimate=moved(8 * depth * rows),
    )(columns)


def split(x):
    high = x.astype(jnp.bfloat16)
    return high, (x - high.astype(jnp.float32)).astype(jnp.bfloat16)


def product_kernel(devices, place_ref, *refs):
    parts, w_hbm = refs[: 2 * devices], refs[2 * devices]
    out_ref, t_ref, w, w_high, w_low, t_high, t_low, arrived = refs[-8:]
    depth, width = w.shape
    block = depth // devices

    @pl.when(pl.program_id(0) == 0)
    def _():
        whole = pltpu.make_async_copy(w_hbm, w, arrived)
        whole.start()
        whole.wait()
        for n in range(devices):
            rows = slice(n * block, (n + 1) * block)
            w_high[rows, :], w_low[rows, :] = split(w[rows, :])

    for n in range(devices):
        value = jnp.concatenate([parts[2 * n][...], parts[2 * n + 1][...]], axis=1)
        to = pl.ds(pl.multiple_of((place_ref[0] ^ n) * block, block), block)
        t_ref[:, to] = value
        t_high[:, to], t_low[:, to] = split(value)
    dot = functools.partial(jnp.dot, preferred_element_type=jnp.float32)
    total = dot(t_low[...], w_high[...])
    total += dot(t_high[...], w_low[...])
    total += dot(t_high[...], w_high[...])
    out_ref[:, :width] = 0.5 * total


def product(place, parts, w, chunk, full):
    start, width, block = chunk
    rows, size = parts[0].shape
    depth = w.shape[0]
    t_half = pltpu.VMEM((ROWS, depth), jnp.bfloat16)
    w_half = pltpu.VMEM((depth, width), jnp.bfloat16)
    return pl.pallas_call(
        functools.partial(product_kernel, len(parts) // 2),
        grid_spec=pltpu.PrefetchScalarGridSpec(
            num_scalar_prefetch=1,
            grid=(pl.cdiv(rows, ROWS),),
            in_specs=[pl.BlockSpec((ROWS, size), lambda i, p: (i, 0))] * len(parts)
            + [pl.BlockSpec(memory_space=pl.ANY)],
            out_specs=[
                pl.BlockSpec((ROWS, block), lambda i, p: (i, start // block)),
                pl.BlockSpec((ROWS, depth), lambda i, p: (i, 0)),
            ],
            scratch_shapes=[
                pltpu.VMEM((depth, width), jnp.float32),
                w_half,
                w_half,
                t_half,
                t_half,
                pltpu.SemaphoreType.DMA(()),
            ],
        ),
        out_shape=[
            jax.ShapeDtypeStruct((rows, full), jnp.float32),
            jax.ShapeDtypeStruct((rows, depth), jnp.float32),
        ],
        compiler_params=params(),
        cost_estimate=moved(
            4 * (2 * rows * depth + depth * width + rows * width),
            6 * rows * depth * width,
        ),
    )(place, *parts, w)


def tie(*values):
    return lax.optimization_barrier(values)


def per_device(line, devices, amplitudes, integrals):
    columns = integrals.shape[1]
    rows = amplitudes.shape[0] // line
    chunks = chunks_of(columns)

    def swap(x, mask):
        return lax.ppermute(x, "ka", [(d, d ^ mask) for d in range(devices)])

    pieces = []
    for start, width, _ in chunks:
        x = lax.slice_in_dim(integrals, start, start + width, axis=1)
        x = x.reshape(devices // line, line, 2, -1, width).swapaxes(1, 2)
        pieces.append(x.reshape(-1, width))

    def gather(x):
        return lax.all_gather(x, "ga", axis=0, tiled=True)

    held = []
    for half in range(2):
        blocks = cut(amplitudes.T, line, half)
        if half:
            blocks, first, *pieces[:2] = tie(blocks, first, *pieces[:2])
            gathered = [gather(x) for x in pieces[:2]]
            held.append({0: turn(first)})
        blocks = lax.all_to_all(blocks, "ga", split_axis=0, concat_axis=0, tiled=True)
        first = blocks.reshape(-1, rows)
    held.append({0: turn(first)})

    masks = [1 << bit for bit in range(1, devices.bit_length() - 1)]
    orders = (masks[::-1], masks)
    across = [{}, {}]
    for half, order in enumerate(orders):
        blocks = held[half]
        if half:
            across[1] = {0: swap(blocks[0], 1)}
        for level in range(1, len(masks) + 1):
            if half and level == 2:
                held, across, pieces = tie(held, across, pieces)
                gathered += [gather(x) for x in pieces[2:]]
                blocks = held[1]
            if half and level == 2 == len(masks):
                some = rows // 16 * 8
                by_first = swap(blocks[masks[0]][:some], masks[1])
                by_second = swap(blocks[masks[1]][some:], masks[0])
                blocks[masks[0] | masks[1]] = jnp.concatenate([by_first, by_second])
                continue
            for n in range(2, devices, 2):
                if n.bit_count() == level:
                    last = [mask for mask in order if n & mask][-1]
                    blocks[n] = swap(blocks[n ^ last], last)
        for n in sorted(blocks.keys() - across[half].keys()):
            across[half][n] = swap(blocks[n], 1)
    parts = [
        (across if n % 2 else held)[half][n - n % 2]
        for n in range(devices)
        for half in range(2)
    ]

    place = lax.axis_index("ka").astype(jnp.int32)
    out, whole = product(place.reshape(1), parts, gathered[0], chunks[0], columns)
    for (start, _, _), w in zip(chunks[1:], gathered[1:]):
        ladder = jnp.dot(
            whole,
            w,
            precision=lax.Precision.HIGH,
            preferred_element_type=jnp.float32,
        )
        out = lax.dynamic_update_slice_in_dim(out, 0.5 * ladder, start, axis=1)
    return out


def solution(mesh):
    placed = (P(None, ("ka", "ga")), P("ga", "ka"))
    return jax.shard_map(
        functools.partial(per_device, mesh.shape["ga"], mesh.shape["ka"]),
        mesh=mesh,
        in_specs=placed,
        out_specs=P("ga", "ka"),
        check_vma=False,
    )
```

```python
import functools

import jax
import jax.numpy as jnp
from jax import lax
from jax.experimental import pallas as pl
from jax.experimental.pallas import tpu as pltpu
from jax.sharding import PartitionSpec as P

ROWS = 240
WIDE = 512
VMEM_BYTES = 60 * 2**20


def params():
    return pltpu.CompilerParams(vmem_limit_bytes=VMEM_BYTES)


def moved(bytes_accessed, flops=0):
    return pl.CostEstimate(
        flops=flops, bytes_accessed=bytes_accessed, transcendentals=0
    )


def chunks_of(columns):
    if columns == 1920:
        order = [(0, 1280), (1280, 512), (1792, 128)]
        return [(start, width, width) for start, width in order]
    wide = [(n, WIDE, WIDE) for n in range(0, columns - WIDE + 1, WIDE)]
    start = len(wide) * WIDE
    return wide + ([(start, columns - start, WIDE)] if start < columns else [])


def cut_kernel(t_ref, out_ref):
    groups, _, rows = out_ref.shape
    for n in range(groups):
        out_ref[n] = t_ref[:, n * rows : (n + 1) * rows]


def cut(columns, groups, half):
    depth, pairs = columns.shape
    shape = (groups, depth // 2, pairs // groups)
    return pl.pallas_call(
        cut_kernel,
        grid=(1,),
        in_specs=[pl.BlockSpec((depth // 2, pairs), lambda i: (half, 0))],
        out_specs=pl.BlockSpec(shape, lambda i: (0, 0, 0)),
        out_shape=jax.ShapeDtypeStruct(shape, jnp.float32),
        compiler_params=params(),
        cost_estimate=moved(4 * depth * pairs),
    )(columns)


def turn_kernel(t_ref, out_ref):
    out_ref[...] = t_ref[...].T


def turn(columns):
    depth, rows = columns.shape
    width = 512
    return pl.pallas_call(
        turn_kernel,
        grid=(pl.cdiv(rows, width),),
        in_specs=[pl.BlockSpec((depth, width), lambda i: (0, i))],
        out_specs=pl.BlockSpec((width, depth), lambda i: (i, 0)),
        out_shape=jax.ShapeDtypeStruct((rows, depth), jnp.float32),
        compiler_params=params(),
        cost_estimate=moved(8 * depth * rows),
    )(columns)


def split(x):
    high = x.astype(jnp.bfloat16)
    return high, (x - high.astype(jnp.float32)).astype(jnp.bfloat16)


def product_kernel(devices, place_ref, *refs):
    parts, w_hbm = refs[: 2 * devices], refs[2 * devices]
    out_ref, t_ref, w, w_high, w_low, t_high, t_low, arrived = refs[-8:]
    depth, width = w.shape
    block = depth // devices

    @pl.when(pl.program_id(0) == 0)
    def _():
        whole = pltpu.make_async_copy(w_hbm, w, arrived)
        whole.start()
        whole.wait()
        for n in range(devices):
            rows = slice(n * block, (n + 1) * block)
            w_high[rows, :], w_low[rows, :] = split(w[rows, :])

    for n in range(devices):
        value = jnp.concatenate([parts[2 * n][...], parts[2 * n + 1][...]], axis=1)
        to = pl.ds(pl.multiple_of((place_ref[0] ^ n) * block, block), block)
        t_ref[:, to] = value
        t_high[:, to], t_low[:, to] = split(value)
    dot = functools.partial(jnp.dot, preferred_element_type=jnp.float32)
    total = dot(t_low[...], w_high[...])
    total += dot(t_high[...], w_low[...])
    total += dot(t_high[...], w_high[...])
    out_ref[:, :width] = 0.5 * total


def product(place, parts, w, chunk, full):
    start, width, block = chunk
    rows, size = parts[0].shape
    depth = w.shape[0]
    t_half = pltpu.VMEM((ROWS, depth), jnp.bfloat16)
    w_half = pltpu.VMEM((depth, width), jnp.bfloat16)
    return pl.pallas_call(
        functools.partial(product_kernel, len(parts) // 2),
        grid_spec=pltpu.PrefetchScalarGridSpec(
            num_scalar_prefetch=1,
            grid=(pl.cdiv(rows, ROWS),),
            in_specs=[pl.BlockSpec((ROWS, size), lambda i, p: (i, 0))] * len(parts)
            + [pl.BlockSpec(memory_space=pl.ANY)],
            out_specs=[
                pl.BlockSpec((ROWS, block), lambda i, p: (i, start // block)),
                pl.BlockSpec((ROWS, depth), lambda i, p: (i, 0)),
            ],
            scratch_shapes=[
                pltpu.VMEM((depth, width), jnp.float32),
                w_half,
                w_half,
                t_half,
                t_half,
                pltpu.SemaphoreType.DMA(()),
            ],
        ),
        out_shape=[
            jax.ShapeDtypeStruct((rows, full), jnp.float32),
            jax.ShapeDtypeStruct((rows, depth), jnp.float32),
        ],
        compiler_params=params(),
        cost_estimate=moved(
            4 * (2 * rows * depth + depth * width + rows * width),
            6 * rows * depth * width,
        ),
    )(place, *parts, w)


def tie(*values):
    return lax.optimization_barrier(values)


def per_device(line, devices, amplitudes, integrals):
    columns = integrals.shape[1]
    rows = amplitudes.shape[0] // line
    chunks = chunks_of(columns)

    def swap(x, mask):
        return lax.ppermute(x, "ka", [(d, d ^ mask) for d in range(devices)])

    def piece(n, source):
        start, width, _ = chunks[n]
        x = lax.slice_in_dim(source, start, start + width, axis=1)
        x = x.reshape(devices // line, line, 2, -1, width).swapaxes(1, 2)
        return x.reshape(-1, width)

    def gather(x):
        return lax.all_gather(x, "ga", axis=0, tiled=True)

    held = []
    for half in range(2):
        blocks = cut(amplitudes.T, line, half)
        if half:
            now = piece(0, integrals)
            blocks, first, now, source = tie(blocks, first, now, integrals)
            gathered = [gather(now)]
            first, then = tie(first, piece(1, source))
            gathered.append(gather(then))
            held.append({0: turn(first)})
        blocks = lax.all_to_all(blocks, "ga", split_axis=0, concat_axis=0, tiled=True)
        first = blocks.reshape(-1, rows)
    held.append({0: turn(first)})

    masks = [1 << bit for bit in range(1, devices.bit_length() - 1)]
    orders = (masks[::-1], masks)
    across = [{}, {}]
    for half, order in enumerate(orders):
        blocks = held[half]
        if half:
            across[1] = {0: swap(blocks[0], 1)}
        for level in range(1, len(masks) + 1):
            if half and level == 2:
                held, across, source = tie(held, across, integrals)
                gathered += [gather(piece(n, source)) for n in range(2, len(chunks))]
                blocks = held[1]
            if half and level == 2 == len(masks):
                some = rows // 16 * 8
                by_first = swap(blocks[masks[0]][:some], masks[1])
                by_second = swap(blocks[masks[1]][some:], masks[0])
                blocks[masks[0] | masks[1]] = jnp.concatenate([by_first, by_second])
                continue
            for n in range(2, devices, 2):
                if n.bit_count() == level:
                    last = [mask for mask in order if n & mask][-1]
                    blocks[n] = swap(blocks[n ^ last], last)
        for n in sorted(blocks.keys() - across[half].keys()):
            across[half][n] = swap(blocks[n], 1)
    parts = [
        (across if n % 2 else held)[half][n - n % 2]
        for n in range(devices)
        for half in range(2)
    ]

    place = lax.axis_index("ka").astype(jnp.int32)
    out, whole = product(place.reshape(1), parts, gathered[0], chunks[0], columns)
    for (start, _, _), w in zip(chunks[1:], gathered[1:]):
        ladder = jnp.dot(
            whole,
            w,
            precision=lax.Precision.HIGH,
            preferred_element_type=jnp.float32,
        )
        out = lax.dynamic_update_slice_in_dim(out, 0.5 * ladder, start, axis=1)
    return out


def solution(mesh):
    placed = (P(None, ("ka", "ga")), P("ga", "ka"))
    return jax.shard_map(
        functools.partial(per_device, mesh.shape["ga"], mesh.shape["ka"]),
        mesh=mesh,
        in_specs=placed,
        out_specs=P("ga", "ka"),
        check_vma=False,
    )
```

```python
import functools

import jax
import jax.numpy as jnp
from jax import lax
from jax.experimental import pallas as pl
from jax.experimental.pallas import tpu as pltpu
from jax.sharding import PartitionSpec as P

ROWS = 240
WIDE = 512
VMEM_BYTES = 60 * 2**20


def params():
    return pltpu.CompilerParams(vmem_limit_bytes=VMEM_BYTES)


def moved(bytes_accessed, flops=0):
    return pl.CostEstimate(
        flops=flops, bytes_accessed=bytes_accessed, transcendentals=0
    )


def chunks_of(columns):
    if columns == 1920:
        order = [(0, 1024), (1024, 128), (1152, 512), (1664, 256)]
        return [(start, width, width) for start, width in order]
    wide = [(n, WIDE, WIDE) for n in range(0, columns - WIDE + 1, WIDE)]
    start = len(wide) * WIDE
    return wide + ([(start, columns - start, WIDE)] if start < columns else [])


def cut_kernel(t_ref, out_ref):
    groups, _, rows = out_ref.shape
    for n in range(groups):
        out_ref[n] = t_ref[:, n * rows : (n + 1) * rows]


def cut(columns, groups, half):
    depth, pairs = columns.shape
    shape = (groups, depth // 2, pairs // groups)
    return pl.pallas_call(
        cut_kernel,
        grid=(1,),
        in_specs=[pl.BlockSpec((depth // 2, pairs), lambda i: (half, 0))],
        out_specs=pl.BlockSpec(shape, lambda i: (0, 0, 0)),
        out_shape=jax.ShapeDtypeStruct(shape, jnp.float32),
        compiler_params=params(),
        cost_estimate=moved(4 * depth * pairs),
    )(columns)


def turn_kernel(t_ref, out_ref):
    out_ref[...] = t_ref[...].T


def turn(columns):
    depth, rows = columns.shape
    width = 512
    return pl.pallas_call(
        turn_kernel,
        grid=(pl.cdiv(rows, width),),
        in_specs=[pl.BlockSpec((depth, width), lambda i: (0, i))],
        out_specs=pl.BlockSpec((width, depth), lambda i: (i, 0)),
        out_shape=jax.ShapeDtypeStruct((rows, depth), jnp.float32),
        compiler_params=params(),
        cost_estimate=moved(8 * depth * rows),
    )(columns)


def split(x):
    high = x.astype(jnp.bfloat16)
    return high, (x - high.astype(jnp.float32)).astype(jnp.bfloat16)


def product_kernel(devices, place_ref, *refs):
    parts, w_hbm = refs[: 2 * devices], refs[2 * devices]
    out_ref, t_ref, w, w_high, w_low, t_high, t_low, arrived = refs[-8:]
    depth, width = w.shape
    block = depth // devices

    @pl.when(pl.program_id(0) == 0)
    def _():
        whole = pltpu.make_async_copy(w_hbm, w, arrived)
        whole.start()
        whole.wait()
        for n in range(devices):
            rows = slice(n * block, (n + 1) * block)
            w_high[rows, :], w_low[rows, :] = split(w[rows, :])

    for n in range(devices):
        value = jnp.concatenate([parts[2 * n][...], parts[2 * n + 1][...]], axis=1)
        to = pl.ds(pl.multiple_of((place_ref[0] ^ n) * block, block), block)
        t_ref[:, to] = value
        t_high[:, to], t_low[:, to] = split(value)
    dot = functools.partial(jnp.dot, preferred_element_type=jnp.float32)
    total = dot(t_low[...], w_high[...])
    total += dot(t_high[...], w_low[...])
    total += dot(t_high[...], w_high[...])
    out_ref[:, :width] = 0.5 * total


def product(place, parts, w, chunk, full):
    start, width, block = chunk
    rows, size = parts[0].shape
    depth = w.shape[0]
    t_half = pltpu.VMEM((ROWS, depth), jnp.bfloat16)
    w_half = pltpu.VMEM((depth, width), jnp.bfloat16)
    return pl.pallas_call(
        functools.partial(product_kernel, len(parts) // 2),
        grid_spec=pltpu.PrefetchScalarGridSpec(
            num_scalar_prefetch=1,
            grid=(pl.cdiv(rows, ROWS),),
            in_specs=[pl.BlockSpec((ROWS, size), lambda i, p: (i, 0))] * len(parts)
            + [pl.BlockSpec(memory_space=pl.ANY)],
            out_specs=[
                pl.BlockSpec((ROWS, block), lambda i, p: (i, start // block)),
                pl.BlockSpec((ROWS, depth), lambda i, p: (i, 0)),
            ],
            scratch_shapes=[
                pltpu.VMEM((depth, width), jnp.float32),
                w_half,
                w_half,
                t_half,
                t_half,
                pltpu.SemaphoreType.DMA(()),
            ],
        ),
        out_shape=[
            jax.ShapeDtypeStruct((rows, full), jnp.float32),
            jax.ShapeDtypeStruct((rows, depth), jnp.float32),
        ],
        compiler_params=params(),
        cost_estimate=moved(
            4 * (2 * rows * depth + depth * width + rows * width),
            6 * rows * depth * width,
        ),
    )(place, *parts, w)


def tie(*values):
    return lax.optimization_barrier(values)


def per_device(line, devices, amplitudes, integrals):
    columns = integrals.shape[1]
    rows = amplitudes.shape[0] // line
    chunks = chunks_of(columns)

    def swap(x, mask):
        return lax.ppermute(x, "ka", [(d, d ^ mask) for d in range(devices)])

    def piece(n, source):
        start, width, _ = chunks[n]
        x = lax.slice_in_dim(source, start, start + width, axis=1)
        x = x.reshape(devices // line, line, 2, -1, width).swapaxes(1, 2)
        return x.reshape(-1, width)

    def gather(x):
        return lax.all_gather(x, "ga", axis=0, tiled=True)

    narrow = []
    if len(chunks) > 2:
        now, amplitudes = tie(piece(1, integrals), amplitudes)
        narrow = [gather(now)]

    held = []
    for half in range(2):
        blocks = cut(amplitudes.T, line, half)
        if half:
            now = piece(0, integrals)
            blocks, first, now, source, narrow = tie(
                blocks, first, now, integrals, narrow
            )
            gathered = [gather(now), *narrow]
            first, then = tie(first, piece(len(gathered), source))
            gathered.append(gather(then))
            held.append({0: turn(first)})
        blocks = lax.all_to_all(blocks, "ga", split_axis=0, concat_axis=0, tiled=True)
        first = blocks.reshape(-1, rows)
    held.append({0: turn(first)})

    masks = [1 << bit for bit in range(1, devices.bit_length() - 1)]
    orders = (masks[::-1], masks)
    across = [{}, {}]
    for half, order in enumerate(orders):
        blocks = held[half]
        if half:
            across[1] = {0: swap(blocks[0], 1)}
        for level in range(1, len(masks) + 1):
            if half and level == 2:
                held, across, source = tie(held, across, integrals)
                gathered += [gather(piece(n, source)) for n in range(len(gathered), len(chunks))]
                blocks = held[1]
            if half and level == 2 == len(masks):
                some = rows // 16 * 8
                by_first = swap(blocks[masks[0]][:some], masks[1])
                by_second = swap(blocks[masks[1]][some:], masks[0])
                blocks[masks[0] | masks[1]] = jnp.concatenate([by_first, by_second])
                continue
            for n in range(2, devices, 2):
                if n.bit_count() == level:
                    last = [mask for mask in order if n & mask][-1]
                    blocks[n] = swap(blocks[n ^ last], last)
        for n in sorted(blocks.keys() - across[half].keys()):
            across[half][n] = swap(blocks[n], 1)
    parts = [
        (across if n % 2 else held)[half][n - n % 2]
        for n in range(devices)
        for half in range(2)
    ]

    place = lax.axis_index("ka").astype(jnp.int32)
    out, whole = product(place.reshape(1), parts, gathered[0], chunks[0], columns)
    for (start, _, _), w in zip(chunks[1:], gathered[1:]):
        ladder = jnp.dot(
            whole,
            w,
            precision=lax.Precision.HIGH,
            preferred_element_type=jnp.float32,
        )
        out = lax.dynamic_update_slice_in_dim(out, 0.5 * ladder, start, axis=1)
    return out


def solution(mesh):
    placed = (P(None, ("ka", "ga")), P("ga", "ka"))
    return jax.shard_map(
        functools.partial(per_device, mesh.shape["ga"], mesh.shape["ka"]),
        mesh=mesh,
        in_specs=placed,
        out_specs=P("ga", "ka"),
        check_vma=False,
    )
```

```python
import functools

import jax
import jax.numpy as jnp
from jax import lax
from jax.experimental import pallas as pl
from jax.experimental.pallas import tpu as pltpu
from jax.sharding import PartitionSpec as P

ROWS = 240
WIDE = 512
VMEM_BYTES = 60 * 2**20


def params():
    return pltpu.CompilerParams(vmem_limit_bytes=VMEM_BYTES)


def moved(bytes_accessed, flops=0):
    return pl.CostEstimate(
        flops=flops, bytes_accessed=bytes_accessed, transcendentals=0
    )


def chunks_of(columns):
    if columns == 1920:
        order = [(0, 1024), (1280, 640), (1024, 256)]
        return [(start, width, width) for start, width in order]
    wide = [(n, WIDE, WIDE) for n in range(0, columns - WIDE + 1, WIDE)]
    start = len(wide) * WIDE
    return wide + ([(start, columns - start, WIDE)] if start < columns else [])


def cut_kernel(t_ref, out_ref):
    groups, _, rows = out_ref.shape
    for n in range(groups):
        out_ref[n] = t_ref[:, n * rows : (n + 1) * rows]


def cut(columns, groups, half):
    depth, pairs = columns.shape
    shape = (groups, depth // 2, pairs // groups)
    return pl.pallas_call(
        cut_kernel,
        grid=(1,),
        in_specs=[pl.BlockSpec((depth // 2, pairs), lambda i: (half, 0))],
        out_specs=pl.BlockSpec(shape, lambda i: (0, 0, 0)),
        out_shape=jax.ShapeDtypeStruct(shape, jnp.float32),
        compiler_params=params(),
        cost_estimate=moved(4 * depth * pairs),
    )(columns)


def turn_kernel(t_ref, out_ref):
    out_ref[...] = t_ref[...].T


def turn(columns):
    depth, rows = columns.shape
    width = 512
    return pl.pallas_call(
        turn_kernel,
        grid=(pl.cdiv(rows, width),),
        in_specs=[pl.BlockSpec((depth, width), lambda i: (0, i))],
        out_specs=pl.BlockSpec((width, depth), lambda i: (i, 0)),
        out_shape=jax.ShapeDtypeStruct((rows, depth), jnp.float32),
        compiler_params=params(),
        cost_estimate=moved(8 * depth * rows),
    )(columns)


def split(x):
    high = x.astype(jnp.bfloat16)
    return high, (x - high.astype(jnp.float32)).astype(jnp.bfloat16)


def product_kernel(halves, added, place_ref, *refs):
    out_ref, w, w_high, w_low, t_high, t_low, arrived = refs[-7:]
    count = arrived.shape[0]
    parts, w_hbm = refs[:count], refs[count]
    size = w.shape[0] // count

    @pl.when(pl.program_id(0) == 0)
    def _():
        copies = []
        for n in range(count):
            block = place_ref[0] ^ (n // len(halves))
            start = (2 * block + halves[n % len(halves)]) * size
            rows = pl.ds(pl.multiple_of(start, size), size)
            to = w.at[pl.ds(n * size, size)]
            copies.append(pltpu.make_async_copy(w_hbm.at[rows], to, arrived.at[n]))
            copies[-1].start()
        for n, copy in enumerate(copies):
            copy.wait()
        for n in range(count):
            rows = slice(n * size, (n + 1) * size)
            w_high[rows, :], w_low[rows, :] = split(w[rows, :])

    for n, part in enumerate(parts):
        to = slice(n * size, (n + 1) * size)
        t_high[:, to], t_low[:, to] = split(part[...])
    dot = functools.partial(jnp.dot, preferred_element_type=jnp.float32)
    total = dot(t_low[...], w_high[...])
    total += dot(t_high[...], w_low[...])
    total += dot(t_high[...], w_high[...])
    width = w.shape[1]
    if added:
        out_ref[:, :width] = refs[count + 1][:, :width] + 0.5 * total
    else:
        out_ref[:, :width] = 0.5 * total


def product(place, parts, halves, w, out, added, chunk, full):
    start, width, block = chunk
    rows, size = parts[0].shape
    count = len(parts)
    depth = size * count
    anywhere = pl.BlockSpec(memory_space=pl.ANY)
    out_spec = pl.BlockSpec((ROWS, block), lambda i, p: (i, start // block))
    operands = [place, *parts, w]
    in_specs = [pl.BlockSpec((ROWS, size), lambda i, p: (i, 0))] * count + [anywhere]
    aliases = {}
    if out is not None:
        aliases = {len(operands): 0}
        operands.append(out)
        in_specs.append(out_spec if added else anywhere)
    t_half = pltpu.VMEM((ROWS, depth), jnp.bfloat16)
    w_half = pltpu.VMEM((depth, width), jnp.bfloat16)
    return pl.pallas_call(
        functools.partial(product_kernel, halves, added),
        grid_spec=pltpu.PrefetchScalarGridSpec(
            num_scalar_prefetch=1,
            grid=(pl.cdiv(rows, ROWS),),
            in_specs=in_specs,
            out_specs=out_spec,
            scratch_shapes=[
                pltpu.VMEM((depth, width), jnp.float32),
                w_half,
                w_half,
                t_half,
                t_half,
                pltpu.SemaphoreType.DMA((count,)),
            ],
        ),
        out_shape=jax.ShapeDtypeStruct((rows, full), jnp.float32),
        input_output_aliases=aliases,
        compiler_params=params(),
        cost_estimate=moved(
            4 * (rows * depth + depth * width + rows * width),
            6 * rows * depth * width,
        ),
    )(*operands)


def tie(*values):
    return lax.optimization_barrier(values)


def per_device(line, devices, amplitudes, integrals):
    columns = integrals.shape[1]
    rows = amplitudes.shape[0] // line
    chunks = chunks_of(columns)

    def swap(x, mask):
        return lax.ppermute(x, "ka", [(d, d ^ mask) for d in range(devices)])

    def gather(n, source):
        start, width, _ = chunks[n]
        x = lax.slice_in_dim(source, start, start + width, axis=1)
        x = x.reshape(devices // line, line, 2, -1, width).swapaxes(1, 2)
        return lax.all_gather(x.reshape(-1, width), "ga", axis=0, tiled=True)

    source, amplitudes = tie(integrals, amplitudes)
    gathered = [gather(0, source)]

    held = []
    for half in range(2):
        blocks = cut(amplitudes.T, line, half)
        if half:
            blocks, first, source = tie(blocks, first, integrals)
            gathered.append(gather(1, source))
            held.append({0: turn(first)})
        blocks = lax.all_to_all(blocks, "ga", split_axis=0, concat_axis=0, tiled=True)
        first = blocks.reshape(-1, rows)
    held.append({0: turn(first)})

    masks = [1 << bit for bit in range(1, devices.bit_length() - 1)]
    orders = (masks[::-1], masks)
    across = [{}, {}]
    place = lax.axis_index("ka").astype(jnp.int32).reshape(1)

    def parts_of(half):
        both = held[half], across[half]
        return [both[n % 2][n - n % 2] for n in range(devices)]

    for half, order in enumerate(orders):
        blocks = held[half]
        if half:
            across[1] = {0: swap(blocks[0], 1)}
        for level in range(1, len(masks) + 1):
            if half and level == 2:
                out = product(
                    place, parts_of(0), (0,), gathered[0], None, False, chunks[0], columns
                )
                held, across, source, out = tie(held, across, integrals, out)
                gathered += [gather(n, source) for n in range(2, len(chunks))]
                blocks = held[1]
            if half and level == 2 == len(masks):
                some = rows // 16 * 8
                by_first = swap(blocks[masks[0]][:some], masks[1])
                by_second = swap(blocks[masks[1]][some:], masks[0])
                blocks[masks[0] | masks[1]] = jnp.concatenate([by_first, by_second])
                continue
            for n in range(2, devices, 2):
                if n.bit_count() == level:
                    last = [mask for mask in order if n & mask][-1]
                    blocks[n] = swap(blocks[n ^ last], last)
        for n in sorted(blocks.keys() - across[half].keys()):
            across[half][n] = swap(blocks[n], 1)
    out = product(
        place, parts_of(1), (1,), gathered[0], out, True, chunks[0], columns
    )
    parts = [x for pair in zip(parts_of(0), parts_of(1)) for x in pair]
    for chunk, w in zip(chunks[1:], gathered[1:]):
        out = product(place, parts, (0, 1), w, out, False, chunk, columns)
    return out


def solution(mesh):
    placed = (P(None, ("ka", "ga")), P("ga", "ka"))
    return jax.shard_map(
        functools.partial(per_device, mesh.shape["ga"], mesh.shape["ka"]),
        mesh=mesh,
        in_specs=placed,
        out_specs=P("ga", "ka"),
        check_vma=False,
    )
```

```python
import functools

import jax
import jax.numpy as jnp
from jax import lax
from jax.experimental import pallas as pl
from jax.experimental.pallas import tpu as pltpu
from jax.sharding import PartitionSpec as P

ROWS = 240
WIDE = 512
VMEM_BYTES = 60 * 2**20


def params():
    return pltpu.CompilerParams(vmem_limit_bytes=VMEM_BYTES)


def moved(bytes_accessed, flops=0):
    return pl.CostEstimate(
        flops=flops, bytes_accessed=bytes_accessed, transcendentals=0
    )


def chunks_of(columns):
    if columns == 1920:
        order = [(0, 1024), (1280, 640), (1024, 256)]
        return [(start, width, width) for start, width in order]
    wide = [(n, WIDE, WIDE) for n in range(0, columns - WIDE + 1, WIDE)]
    start = len(wide) * WIDE
    return wide + ([(start, columns - start, WIDE)] if start < columns else [])


def cut_kernel(t_ref, out_ref):
    groups, _, rows = out_ref.shape
    for n in range(groups):
        out_ref[n] = t_ref[:, n * rows : (n + 1) * rows]


def cut(columns, groups, half):
    depth, pairs = columns.shape
    shape = (groups, depth // 2, pairs // groups)
    return pl.pallas_call(
        cut_kernel,
        grid=(1,),
        in_specs=[pl.BlockSpec((depth // 2, pairs), lambda i: (half, 0))],
        out_specs=pl.BlockSpec(shape, lambda i: (0, 0, 0)),
        out_shape=jax.ShapeDtypeStruct(shape, jnp.float32),
        compiler_params=params(),
        cost_estimate=moved(4 * depth * pairs),
    )(columns)


def turn_kernel(t_ref, out_ref):
    out_ref[...] = t_ref[...].T


def turn(columns):
    depth, rows = columns.shape
    width = 512
    return pl.pallas_call(
        turn_kernel,
        grid=(pl.cdiv(rows, width),),
        in_specs=[pl.BlockSpec((depth, width), lambda i: (0, i))],
        out_specs=pl.BlockSpec((width, depth), lambda i: (i, 0)),
        out_shape=jax.ShapeDtypeStruct((rows, depth), jnp.float32),
        compiler_params=params(),
        cost_estimate=moved(8 * depth * rows),
    )(columns)


def split(x):
    high = x.astype(jnp.bfloat16)
    return high, (x - high.astype(jnp.float32)).astype(jnp.bfloat16)


def product_kernel(halves, added, place_ref, *refs):
    out_ref, w, w_high, w_low, t_high, t_low, arrived = refs[-7:]
    count = arrived.shape[0]
    parts, w_hbm = refs[:count], refs[count]
    size = w.shape[0] // count

    @pl.when(pl.program_id(0) == 0)
    def _():
        copies = []
        for n in range(count):
            block = place_ref[0] ^ (n // len(halves))
            start = (2 * block + halves[n % len(halves)]) * size
            rows = pl.ds(pl.multiple_of(start, size), size)
            to = w.at[pl.ds(n * size, size)]
            copies.append(pltpu.make_async_copy(w_hbm.at[rows], to, arrived.at[n]))
            copies[-1].start()
        for n, copy in enumerate(copies):
            copy.wait()
        for n in range(count):
            rows = slice(n * size, (n + 1) * size)
            w_high[rows, :], w_low[rows, :] = split(w[rows, :])

    for n, part in enumerate(parts):
        to = slice(n * size, (n + 1) * size)
        t_high[:, to], t_low[:, to] = split(part[...])
    dot = functools.partial(jnp.dot, preferred_element_type=jnp.float32)
    total = dot(t_low[...], w_high[...])
    total += dot(t_high[...], w_low[...])
    total += dot(t_high[...], w_high[...])
    width = w.shape[1]
    if added:
        out_ref[:, :width] = refs[count + 1][:, :width] + 0.5 * total
    else:
        out_ref[:, :width] = 0.5 * total


def product(place, parts, halves, w, out, added, chunk, full):
    start, width, block = chunk
    rows, size = parts[0].shape
    count = len(parts)
    tile = ROWS if width > 256 else 3 * ROWS
    depth = size * count
    anywhere = pl.BlockSpec(memory_space=pl.ANY)
    out_spec = pl.BlockSpec((tile, block), lambda i, p: (i, start // block))
    operands = [place, *parts, w]
    in_specs = [pl.BlockSpec((tile, size), lambda i, p: (i, 0))] * count + [anywhere]
    aliases = {}
    if out is not None:
        aliases = {len(operands): 0}
        operands.append(out)
        in_specs.append(out_spec if added else anywhere)
    t_half = pltpu.VMEM((tile, depth), jnp.bfloat16)
    w_half = pltpu.VMEM((depth, width), jnp.bfloat16)
    return pl.pallas_call(
        functools.partial(product_kernel, halves, added),
        grid_spec=pltpu.PrefetchScalarGridSpec(
            num_scalar_prefetch=1,
            grid=(pl.cdiv(rows, tile),),
            in_specs=in_specs,
            out_specs=out_spec,
            scratch_shapes=[
                pltpu.VMEM((depth, width), jnp.float32),
                w_half,
                w_half,
                t_half,
                t_half,
                pltpu.SemaphoreType.DMA((count,)),
            ],
        ),
        out_shape=jax.ShapeDtypeStruct((rows, full), jnp.float32),
        input_output_aliases=aliases,
        compiler_params=params(),
        cost_estimate=moved(
            4 * (rows * depth + depth * width + rows * width),
            6 * rows * depth * width,
        ),
    )(*operands)


def tie(*values):
    return lax.optimization_barrier(values)


def per_device(line, devices, amplitudes, integrals):
    columns = integrals.shape[1]
    rows = amplitudes.shape[0] // line
    chunks = chunks_of(columns)

    def swap(x, mask):
        return lax.ppermute(x, "ka", [(d, d ^ mask) for d in range(devices)])

    def gather(n, source):
        start, width, _ = chunks[n]
        x = lax.slice_in_dim(source, start, start + width, axis=1)
        x = x.reshape(devices // line, line, 2, -1, width).swapaxes(1, 2)
        return lax.all_gather(x.reshape(-1, width), "ga", axis=0, tiled=True)

    source, amplitudes = tie(integrals, amplitudes)
    gathered = [gather(0, source)]

    held = []
    for half in range(2):
        blocks = cut(amplitudes.T, line, half)
        if half:
            blocks, first, source = tie(blocks, first, integrals)
            gathered.append(gather(1, source))
            held.append({0: turn(first)})
        blocks = lax.all_to_all(blocks, "ga", split_axis=0, concat_axis=0, tiled=True)
        first = blocks.reshape(-1, rows)
    held.append({0: turn(first)})

    masks = [1 << bit for bit in range(1, devices.bit_length() - 1)]
    orders = (masks[::-1], masks)
    across = [{}, {}]
    place = lax.axis_index("ka").astype(jnp.int32).reshape(1)

    def parts_of(half):
        both = held[half], across[half]
        return [both[n % 2][n - n % 2] for n in range(devices)]

    for half, order in enumerate(orders):
        blocks = held[half]
        if half:
            across[1] = {0: swap(blocks[0], 1)}
        for level in range(1, len(masks) + 1):
            if half and level == 2:
                out = product(
                    place, parts_of(0), (0,), gathered[0], None, False, chunks[0], columns
                )
                held, across, source, out = tie(held, across, integrals, out)
                gathered += [gather(n, source) for n in range(2, len(chunks))]
                blocks = held[1]
            if half and level == 2 == len(masks):
                some = rows // 16 * 8
                by_first = swap(blocks[masks[0]][:some], masks[1])
                by_second = swap(blocks[masks[1]][some:], masks[0])
                blocks[masks[0] | masks[1]] = jnp.concatenate([by_first, by_second])
                continue
            for n in range(2, devices, 2):
                if n.bit_count() == level:
                    last = [mask for mask in order if n & mask][-1]
                    blocks[n] = swap(blocks[n ^ last], last)
        for n in sorted(blocks.keys() - across[half].keys()):
            across[half][n] = swap(blocks[n], 1)
    out = product(
        place, parts_of(1), (1,), gathered[0], out, True, chunks[0], columns
    )
    parts = [x for pair in zip(parts_of(0), parts_of(1)) for x in pair]
    for chunk, w in zip(chunks[1:], gathered[1:]):
        out = product(place, parts, (0, 1), w, out, False, chunk, columns)
    return out


def solution(mesh):
    placed = (P(None, ("ka", "ga")), P("ga", "ka"))
    return jax.shard_map(
        functools.partial(per_device, mesh.shape["ga"], mesh.shape["ka"]),
        mesh=mesh,
        in_specs=placed,
        out_specs=P("ga", "ka"),
        check_vma=False,
    )
```
